32 devices in a mesh: dp: 4 (over y, x), fsdp: 8 (over z, core).
Axes of the slice: x: 2, y: 2, z: 4, core: 2. Of those that a mesh axis runs over, the one named last changes fastest.
Arguments:
- tokens: bfloat16 [2, 4096, 768], P(None, ('dp', 'fsdp')), may hold values from -6 to 6
- lengths: int32 [2, 32, 8], P(None, ('dp', 'fsdp')), may hold values from 1 to 96, 128 in all within a row
- ln1_gain: float32 [768], P(('dp', 'fsdp')), may hold values from 0.1 to 1.9
- ln1_shift: float32 [768], P(('dp', 'fsdp')), may hold values from -1.5 to 1.5
- w_qkv: float32 [768, 2304], P(('dp', 'fsdp')), may hold values from -0.21875 to 0.21875
- qv_bias: float32 [1536], P(('dp', 'fsdp')), may hold values from -1.5 to 1.5
- w_out: float32 [768, 768], P(('dp', 'fsdp')), may hold values from -0.875 to 0.875
- out_bias: float32 [768], P(('dp', 'fsdp')), may hold values from -1.5 to 1.5
- ln2_gain: float32 [768], P(('dp', 'fsdp')), may hold values from 0.1 to 1.9
- ln2_shift: float32 [768], P(('dp', 'fsdp')), may hold values from -1.5 to 1.5
- w_fc: float32 [768, 3072], P(('dp', 'fsdp')), may hold values from -0.21875 to 0.21875
- fc_bias: float32 [3072], P(('dp', 'fsdp')), may hold values from -1.5 to 1.5
- w_proj: float32 [3072, 768], P(('dp', 'fsdp')), may hold values from -0.109375 to 0.109375
- proj_bias: float32 [768], P(('dp', 'fsdp')), may hold values from -1.5 to 1.5
- cotangent: bfloat16 [2, 4096, 768], P(None, ('dp', 'fsdp')), may hold values from -6 to 6
Outputs:
- activations: bfloat16 [2, 4096, 768], P(None, ('dp', 'fsdp'))
- token_grad: bfloat16 [2, 4096, 768], P(None, ('dp', 'fsdp'))
- ln1_gain_grad: float32 [768], P(('dp', 'fsdp'))
- ln1_shift_grad: float32 [768], P(('dp', 'fsdp'))
- w_qkv_grad: float32 [768, 2304], P(('dp', 'fsdp'))
- qv_bias_grad: float32 [1536], P(('dp', 'fsdp'))
- w_out_grad: float32 [768, 768], P(('dp', 'fsdp'))
- out_bias_grad: float32 [768], P(('dp', 'fsdp'))
- ln2_gain_grad: float32 [768], P(('dp', 'fsdp'))
- ln2_shift_grad: float32 [768], P(('dp', 'fsdp'))
- w_fc_grad: float32 [768, 3072], P(('dp', 'fsdp'))
- fc_bias_grad: float32 [3072], P(('dp', 'fsdp'))
- w_proj_grad: float32 [3072, 768], P(('dp', 'fsdp'))
- proj_bias_grad: float32 [768], P(('dp', 'fsdp'))
The draws below stay inside these ranges and needn't reach their ends.
Inputs may be any that keep to these rules, and one draw needn't show every extreme that they name: Each row lengths[m, b, :] sums to 128, and its largest entry is exactly 96.
All inputs are finite; a program needn't handle non-finite values.
Results may differ from the reference program's by a relative error of at most 0.018.
Values may be sent and summed in bfloat16 or wider, within the bound.
No kernel may reach another device: no remote copies, remote signals or barrier semaphores. Data moves between devices by JAX's collectives and lax.ppermute only.
A program may use at most 192 MiB of HBM per device.

```python
import math
import jax
import jax.numpy as jnp
import numpy as np
from jax import lax

D = 768
HEADS = 12
HD = 64
FF = 3072
BIN = 128
MICRO = 2
SEQS = 8
MOST = 96
TOKENS = 4096
DEVICES = 32


def block_levels(stream_key, extent, shards, least, top_value):
    level, own = 1.0, jax.random.fold_in(stream_key, 6)
    for dim, parts in shards:
        draws = jnp.exp(jax.random.uniform(jax.random.fold_in(own, dim), (parts,), jnp.float32, least / len(shards), top_value / len(shards)))
        level = level * jnp.repeat(draws, extent[dim] // parts).reshape([-1 if axis == dim else 1 for axis in range(len(extent))])
    return level


def length_profile(count, total, limit, lean):
    weights = [(1 << 20) // math.isqrt(grade ** lean) + 1 for grade in range(2, count + 1)]
    surplus, given = total - limit - (count - 1), [1] * (count - 1)
    while surplus > 0:
        candidates = [i for i in range(count - 1) if given[i] < limit]
        whole, left = sum([weights[i] for i in candidates]), surplus
        for i in candidates:
            more = min(limit - given[i], max(1, left * weights[i] // whole), surplus)
            given[i] = given[i] + more
            surplus = surplus - more
    return np.array([limit] + given)


def uneven(key, number_of, total, limit, skew):
    if number_of == 2:
        one = jax.random.randint(key, (), max(1, total - limit), min(limit, total - 1) + 1)
        return jnp.stack([one, total - one])
    sizes = jnp.asarray(length_profile(number_of, total, limit, skew), jnp.int32)
    pairs = (number_of - 1) // 2
    source_of, sink = sizes[1:1 + 2 * pairs:2], sizes[2:2 + 2 * pairs:2]
    room = jnp.minimum(source_of - 1, limit - sink)
    passed = jax.random.randint(jax.random.fold_in(key, 1), (pairs,), 0, 1 << 20) % (room + 1)
    sizes = sizes.at[1:1 + 2 * pairs:2].set(source_of - passed).at[2:2 + 2 * pairs:2].set(sink + passed)
    return sizes[jax.random.permutation(jax.random.fold_in(key, 2), number_of)]


def gaussian(key, shape, scale, reach, cuts=(), kind=jnp.bfloat16):
    array = scale * jax.random.normal(key, shape, jnp.float32)
    if cuts:
        array = array * block_levels(key, shape, cuts, -0.22, 0.18)
    return jnp.clip(array, -reach, reach).astype(kind)


def setup_inputs(seed: int = 0) -> dict:
    splits = jax.random.split(jax.random.key(seed), 16)
    return {
        "tokens": gaussian(splits[0], (MICRO, TOKENS, D), 1.0, 6.0, ((1, 32),)),
        "lengths": jax.vmap(lambda own: uneven(own, SEQS, BIN, MOST, 2))(jax.random.split(splits[1], MICRO * DEVICES)).reshape((MICRO, DEVICES, SEQS)).astype(jnp.int32),
        "ln1_gain": jnp.clip(1.0 + 0.18 * jax.random.normal(splits[2], (D,), jnp.float32), 0.1, 1.9),
        "ln1_shift": gaussian(splits[3], (D,), 0.3, 1.5, ((0, 32),), jnp.float32),
        "w_qkv": gaussian(splits[4], (D, 3 * D), D ** -0.5, 0.21875, ((0, 32),), jnp.float32),
        "qv_bias": gaussian(splits[5], (2 * D,), 0.3, 1.5, ((0, 32),), jnp.float32),
        "w_out": gaussian(splits[6], (D, D), (D // 16) ** -0.5, 0.875, ((0, 32),), jnp.float32),
        "out_bias": gaussian(splits[7], (D,), 0.3, 1.5, ((0, 32),), jnp.float32),
        "ln2_gain": jnp.clip(1.0 + 0.18 * jax.random.normal(splits[8], (D,), jnp.float32), 0.1, 1.9),
        "ln2_shift": gaussian(splits[9], (D,), 0.3, 1.5, ((0, 32),), jnp.float32),
        "w_fc": gaussian(splits[10], (D, FF), D ** -0.5, 0.21875, ((0, 32),), jnp.float32),
        "fc_bias": gaussian(splits[11], (FF,), 0.3, 1.5, ((0, 32),), jnp.float32),
        "w_proj": gaussian(splits[12], (FF, D), FF ** -0.5, 0.109375, ((0, 32),), jnp.float32),
        "proj_bias": gaussian(splits[13], (D,), 0.3, 1.5, ((0, 32),), jnp.float32),
        "cotangent": gaussian(splits[14], (MICRO, TOKENS, D), 1.0, 6.0, ((1, 32),)),
    }


@jax.custom_vjp
def low(v):
    return lax.optimization_barrier(v.astype(jnp.bfloat16)).astype(jnp.float32)

@jax.custom_vjp
def low_back(v):
    return v

def low_keep(v):
    return (low(v), None)

def low_pass(kept, grad):
    return (grad,)

def back_keep(v):
    return (v, None)

def back_low(kept, grad):
    return (low(grad),)
low.defvjp(low_keep, low_pass)
low_back.defvjp(back_keep, back_low)
epsilon = 1e-05
neg_large = -1e+30
highest = lax.Precision.HIGHEST

def norm_rows(hidden, gain_row, shift_row):
    centred = hidden - lax.optimization_barrier(jnp.mean(hidden, axis=-1, keepdims=True))
    spread = lax.optimization_barrier(jnp.mean(centred * centred, axis=-1, keepdims=True))
    return centred * lax.rsqrt(spread + epsilon) * gain_row + shift_row

def gelu_tanh(values):
    return jax.nn.gelu(values, approximate=True)

def allowed_pairs(bin_lengths, row_count):
    segment_ends = jnp.cumsum(bin_lengths, axis=-1)
    places = jnp.arange(row_count, dtype=jnp.int32)
    segment = lax.optimization_barrier(jnp.sum((places[None, :, None] >= segment_ends[:, None, :]).astype(jnp.int32), axis=-1))
    same_segment = segment[:, :, None] == segment[:, None, :]
    return jnp.logical_and(same_segment, places[None, None, :] <= places[None, :, None])

def block_forward(hidden, weights, allowed):
    gain_one, shift_one, w_mixed, mixed_bias, w_attn, attn_bias, gain_two, shift_two, w_up, up_bias, w_down, down_bias = weights
    model_width = hidden.shape[-1]
    bin_count, row_count = (hidden.shape[0], hidden.shape[1])
    score_scale = HD ** (-0.5)
    normed = low(norm_rows(hidden, gain_one, shift_one))
    bias_full = jnp.concatenate([mixed_bias[:model_width], jnp.zeros((model_width,), jnp.float32), mixed_bias[model_width:]])
    mixed_rows = low(low_back(jnp.einsum('btd,de->bte', normed, w_mixed, precision=highest) + bias_full))
    split_rows = mixed_rows.reshape(bin_count, row_count, 3, HEADS, HD)
    query_rows, key_rows, value_rows = (split_rows[:, :, 0], split_rows[:, :, 1], split_rows[:, :, 2])
    scores = low_back(jnp.einsum('bqhe,bkhe->bhqk', query_rows, key_rows, precision=highest) * score_scale)
    masked = jnp.where(allowed[:, None], scores, neg_large)
    row_max = lax.optimization_barrier(jnp.max(masked, axis=-1, keepdims=True))
    exponent = jnp.exp(masked - row_max)
    probabilities = low(exponent / lax.optimization_barrier(jnp.sum(exponent, axis=-1, keepdims=True)))
    attended = jnp.einsum('bhqk,bkhe->bqhe', probabilities, value_rows, precision=highest)
    attended = low(low_back(attended.reshape(bin_count, row_count, model_width)))
    middle = hidden + low_back(jnp.einsum('btd,de->bte', attended, w_attn, precision=highest) + attn_bias)
    normed_two = low(norm_rows(middle, gain_two, shift_two))
    before = low_back(jnp.einsum('btd,df->btf', normed_two, w_up, precision=highest) + up_bias)
    active = low(gelu_tanh(before))
    return middle + low_back(jnp.einsum('btf,fd->btd', active, w_down, precision=highest) + down_bias)

def reference(tokens, lengths, ln1_gain, ln1_shift, w_qkv, qv_bias, w_out, out_bias, ln2_gain, ln2_shift, w_fc, fc_bias, w_proj, proj_bias, cotangent):
    params = (ln1_gain, ln1_shift, w_qkv, qv_bias, w_out, out_bias, ln2_gain, ln2_shift, w_fc, fc_bias, w_proj, proj_bias)
    group_bins = 16
    groups = MICRO * DEVICES // group_bins
    token_groups = tokens.reshape(groups, group_bins, BIN, D)
    length_groups = lengths.reshape(groups, group_bins, SEQS)
    cotangent_groups = cotangent.reshape(groups, group_bins, BIN, D)

    def one_group(totals, inputs):
        group_tokens, group_lengths, group_cotangent = inputs
        allowed = allowed_pairs(group_lengths, BIN)

        def forward(hidden, weights):
            rounded = tuple((low(member) for member in weights))
            for repeat in range(2):
                hidden = block_forward(hidden, rounded, allowed)
            return hidden
        output, pull_back = jax.vjp(forward, group_tokens.astype(jnp.float32), params)
        grad_tokens, grad_params = pull_back(group_cotangent.astype(jnp.float32))
        totals = jax.tree.map(jnp.add, totals, grad_params)
        return (totals, (output.astype(jnp.bfloat16), grad_tokens.astype(jnp.bfloat16)))
    zeros_start = tuple((jnp.zeros(member.shape, jnp.float32) for member in params))
    totals, (outputs, input_grads) = lax.scan(one_group, zeros_start, (token_groups, length_groups, cotangent_groups))
    activations = outputs.reshape(MICRO, TOKENS, D)
    token_grad = input_grads.reshape(MICRO, TOKENS, D)
    return (activations, token_grad, totals[0], totals[1], totals[2], totals[3], totals[4], totals[5], totals[6], totals[7], totals[8], totals[9], totals[10], totals[11])
```

```python
import functools

import jax
import jax.numpy as jnp
from jax import lax
from jax.experimental import pallas as pl
from jax.experimental.pallas import tpu as pltpu
from jax.sharding import PartitionSpec as P

HEADS = 12
HD = 64
EPS = 1e-05
NEG = -1e30
AXES = ("dp", "fsdp")
F32 = jnp.float32
BF16 = jnp.bfloat16
GELU_A = 0.7978845608028654
GELU_B = 0.044715

NT = (((1,), (1,)), ((), ()))
TN = (((0,), (0,)), ((), ()))
NN = (((1,), (0,)), ((), ()))

CYCLE = [(0, 0), (0, 1), (0, 2), (0, 3), (1, 3), (1, 2), (1, 1), (1, 0)]
OFFSETS = (4, 3, -3, 2, -2, 1, -1, 0)
BATCHES = ((4,), (3, -3), (2, -2), (1, -1), (0,))


def place(core, u, o, z):
    x, y = (o, u) if core == 0 else (u, o)
    return (y * 2 + x) * 4 + z


def device_of(chip, core):
    return chip * 2 + core


def ring_pairs(step):
    pairs = []
    for core in range(2):
        for o in range(2):
            for i, (u, z) in enumerate(CYCLE):
                u2, z2 = CYCLE[(i + step) % 8]
                pairs.append((device_of(place(core, u, o, z), core), device_of(place(core, u2, o, z2), core)))
    return pairs


def swap_pairs():
    pairs = []
    for core in range(2):
        for o in range(2):
            for u, z in CYCLE:
                pairs.append((device_of(place(core, u, o, z), core), device_of(place(core, u, 1 - o, z), core)))
    return pairs


def core_pairs():
    return [(d, d ^ 1) for d in range(32)]


def relative_chips(sign):
    table = [[[[0, 0] for _ in OFFSETS] for _ in range(2)] for _ in range(16)]
    for core in range(2):
        for o in range(2):
            for i, (u, z) in enumerate(CYCLE):
                me = place(core, u, o, z)
                for slot, off in enumerate(OFFSETS):
                    u2, z2 = CYCLE[(i + sign * off) % 8]
                    for flip in range(2):
                        table[me][core][slot][flip] = place(core, u2, o ^ flip, z2)
    return table


def dot(a, b, dims):
    return lax.dot_general(a, b, dims, preferred_element_type=F32)


SMALL = dict(g1=0, s1=1, qb=2, vb=3, ob=4, g2=5, s2=6, fb=7, pb=11)

def compute(len_ref, tok_ref, cot_ref, sm_ref, act_ref, tg_ref, sg_ref, scr, loaders, ready, emit):
    wide, proj = loaders
    (a_all, att_all, c_all, ga_all, pre_all, mix_all, h_all, mid_all, prob_all,
     gd_all, gb_all, dpre_all, dmix_all, hid, acc, datt, tmp) = scr
    rows, width = tok_ref.shape
    bins = len_ref.shape[0]
    n = rows // bins
    chunk = 32
    chunks = rows // chunk

    def small(name):
        return sm_ref[:, SMALL[name] * width:(SMALL[name] + 1) * width]

    def add_small(name, value):
        ks = slice(SMALL[name] * width, (SMALL[name] + 1) * width)
        sg_ref[:, ks] = sg_ref[:, ks] + value

    def fc_cols(i):
        return pl.ds(pl.multiple_of((SMALL["fb"] + i) * width, 128), width)

    def at(base, r):
        return pl.ds(pl.multiple_of(base + r * chunk, chunk), chunk)

    sg_ref[...] = jnp.zeros_like(sg_ref)
    low_half = lax.broadcasted_iota(jnp.int32, (n, 2 * HD), 1) < HD
    row_i = lax.broadcasted_iota(jnp.int32, (n, n), 0)
    col_i = lax.broadcasted_iota(jnp.int32, (n, n), 1)
    allowed = []
    for m in range(bins):
        seg_r = jnp.zeros((n, n), jnp.int32)
        seg_c = jnp.zeros((n, n), jnp.int32)
        end = jnp.int32(0)
        for i in range(len_ref.shape[1]):
            end = end + len_ref[m, i]
            seg_r += (row_i >= end).astype(jnp.int32)
            seg_c += (col_i >= end).astype(jnp.int32)
        allowed.append(jnp.logical_and(seg_r == seg_c, col_i <= row_i))

    def halves(v):
        zero = jnp.zeros_like(v)
        return jnp.where(low_half, v, zero), jnp.where(low_half, zero, v)

    def join(parts):
        return jnp.where(low_half, parts[0], parts[1])

    def norm_rows(v):
        cen = v - jnp.mean(v, axis=-1, keepdims=True)
        rstd = lax.rsqrt(jnp.mean(cen * cen, axis=-1, keepdims=True) + EPS)
        return cen * rstd, rstd

    def forward_norm(src, base, gain, shift, dst):
        @pl.loop(0, chunks)
        def _(r):
            xhat, _ = norm_rows(src[at(base, r), :])
            dst[at(base, r), :] = (xhat * gain + shift).astype(BF16)

    def backward_norm(src, base, gain, names, dst16, dst_base):
        def step(r, sums):
            xhat, rstd = norm_rows(src[at(base, r), :])
            dy = acc[at(0, r), :]
            dx = dy * gain
            m1 = jnp.mean(dx, axis=-1, keepdims=True)
            m2 = jnp.mean(dx * xhat, axis=-1, keepdims=True)
            total = hid[at(0, r), :] + rstd * (dx - m1 - xhat * m2)
            hid[at(0, r), :] = total
            dst16[at(dst_base, r), :] = total.astype(BF16)
            return sums[0] + jnp.sum(dy * xhat, axis=0, keepdims=True), sums[1] + jnp.sum(dy, axis=0, keepdims=True)
        zero = jnp.zeros((1, width), F32)
        sums = lax.fori_loop(0, chunks, step, (zero, zero))
        add_small(names[0], sums[0])
        add_small(names[1], sums[1])

    def colsum(v16):
        return jnp.sum(v16.astype(F32), axis=0, keepdims=True)

    def forward(b):
        base = b * rows
        rs = slice(base, base + rows)
        forward_norm(h_all, base, small("g1"), small("s1"), a_all)
        ready("qo")
        mix_all[0, rs, :] = (dot(a_all[rs, :], wide(0), NN) + small("qb")).astype(BF16)
        mix_all[1, rs, :] = dot(a_all[rs, :], wide(1), NN).astype(BF16)
        mix_all[2, rs, :] = (dot(a_all[rs, :], wide(2), NN) + small("vb")).astype(BF16)

        @pl.loop(0, HEADS // 2)
        def _(hp):
            ls = pl.ds(pl.multiple_of(hp * 2 * HD, 2 * HD), 2 * HD)
            for m in range(bins):
                rm = slice(base + m * n, base + (m + 1) * n)
                q2, k2, v2 = (mix_all[j, rm, ls] for j in range(3))
                parts = []
                for half, qh in enumerate(halves(q2)):
                    s = jnp.where(allowed[m], dot(qh, k2, NT) * (HD ** -0.5), NEG)
                    e = jnp.exp(s - jnp.max(s, axis=-1, keepdims=True))
                    p = e / jnp.sum(e, axis=-1, keepdims=True)
                    prob_all[(b * bins + m) * HEADS + hp * 2 + half] = p
                    parts.append(dot(p.astype(BF16), v2, NN))
                att_all[rm, ls] = join(parts).astype(BF16)

        mid_all[rs, :] = h_all[rs, :] + (dot(att_all[rs, :], wide(3), NN) + small("ob"))
        forward_norm(mid_all, base, small("g2"), small("s2"), c_all)
        acc[...] = mid_all[rs, :] + small("pb")
        ready("f")
        ready("p")

        @pl.loop(0, 4)
        def _(i):
            pre_all[i, rs, :] = dot(c_all[rs, :], wide(4 + i), NN) + sm_ref[:, fc_cols(i)]

            @pl.loop(0, chunks)
            def _(r):
                v = pre_all[i, at(base, r), :]
                t = jnp.tanh(GELU_A * (v + GELU_B * (v * v * v)))
                ga_all[i, at(base, r), :] = (0.5 * v * (1.0 + t)).astype(BF16)
            acc[...] += dot(ga_all[i, rs, :], proj(i), NN)

    def backward(b):
        base = b * rows
        rs = slice(base, base + rows)
        add_small("pb", colsum(gd_all[rs, :]))
        acc[...] = jnp.zeros_like(acc)

        @pl.loop(0, 4)
        def _(i):
            tmp[...] = dot(gd_all[rs, :], proj(i), NT)

            def step(r, total):
                v = pre_all[i, at(base, r), :]
                v2 = v * v
                t = jnp.tanh(GELU_A * (v + GELU_B * (v * v2)))
                slope = 0.5 * (1.0 + t) + (0.5 * v) * (1.0 - t * t) * (GELU_A * (1.0 + 3.0 * GELU_B * v2))
                d = (tmp[at(0, r), :] * slope).astype(BF16)
                dpre_all[i, at(base, r), :] = d
                return total + colsum(d)
            total = lax.fori_loop(0, chunks, step, jnp.zeros((1, width), F32))
            sg_ref[:, fc_cols(i)] = sg_ref[:, fc_cols(i)] + total
            acc[...] += dot(dpre_all[i, rs, :], wide(4 + i), NT)

        backward_norm(mid_all, base, small("g2"), ("g2", "s2"), gb_all, base)
        add_small("ob", colsum(gb_all[rs, :]))
        datt[...] = dot(gb_all[rs, :], wide(3), NT).astype(BF16)

        @pl.loop(0, HEADS // 2)
        def _(hp):
            ls = pl.ds(pl.multiple_of(hp * 2 * HD, 2 * HD), 2 * HD)
            for m in range(bins):
                rm = slice(base + m * n, base + (m + 1) * n)
                q2, k2, v2 = (mix_all[j, rm, ls] for j in range(3))
                d2 = datt[m * n:(m + 1) * n, ls]
                dq, dk, dv = [], [], []
                for half, dh in enumerate(halves(d2)):
                    p = prob_all[(b * bins + m) * HEADS + hp * 2 + half]
                    dp = dot(dh, v2, NT)
                    dv.append(dot(p.astype(BF16), d2, TN))
                    ds = (p * (dp - jnp.sum(p * dp, axis=-1, keepdims=True))).astype(BF16)
                    dq.append(dot(ds, k2, NN))
                    dk.append(dot(ds, q2, TN))
                dmix_all[0, rm, ls] = (join(dq) * (HD ** -0.5)).astype(BF16)
                dmix_all[1, rm, ls] = (join(dk) * (HD ** -0.5)).astype(BF16)
                dmix_all[2, rm, ls] = join(dv).astype(BF16)

        add_small("qb", colsum(dmix_all[0, rs, :]))
        add_small("vb", colsum(dmix_all[2, rs, :]))
        acc[...] = dot(dmix_all[0, rs, :], wide(0), NT)
        acc[...] += dot(dmix_all[1, rs, :], wide(1), NT)
        acc[...] += dot(dmix_all[2, rs, :], wide(2), NT)
        backward_norm(h_all, base, small("g1"), ("g1", "s1"), gd_all if b == 1 else tg_ref, 0)

    h_all[0:rows, :] = tok_ref[...].astype(F32)
    forward(0)
    h_all[rows:2 * rows, :] = acc[...]
    forward(1)
    act_ref[...] = acc[...].astype(BF16)
    hid[...] = cot_ref[...].astype(F32)
    gd_all[rows:2 * rows, :] = cot_ref[...]
    backward(1)
    backward(0)
    emit(a_all, att_all, c_all, ga_all, dmix_all, gb_all, dpre_all, gd_all)


def compute_scratch(rows, width):
    two = 2 * rows
    return [
        pltpu.VMEM((two, width), BF16),
        pltpu.VMEM((two, width), BF16),
        pltpu.VMEM((two, width), BF16),
        pltpu.VMEM((4, two, width), BF16),
        pltpu.VMEM((4, two, width), F32),
        pltpu.VMEM((3, two, width), BF16),
        pltpu.VMEM((two, width), F32),
        pltpu.VMEM((two, width), F32),
        pltpu.VMEM((4 * HEADS, rows // 2, rows // 2), F32),
        pltpu.VMEM((two, width), BF16),
        pltpu.VMEM((two, width), BF16),
        pltpu.VMEM((4, two, width), BF16),
        pltpu.VMEM((3, two, width), BF16),
        pltpu.VMEM((rows, width), F32),
        pltpu.VMEM((rows, width), F32),
        pltpu.VMEM((rows, width), BF16),
        pltpu.VMEM((rows, width), F32),
    ]


N_SCR = 17
LIMIT = 64 * 1024 * 1024


def kernel(fast, n_in, n_out, *refs):
    tab, len_ref, tok_ref, cot_ref, sm_ref = refs[:5]
    w_in = refs[5:n_in]
    act_ref, tg_ref, sg_ref = refs[n_in:n_in + 3]
    d_out = refs[n_in + 3:n_in + n_out]
    scr = refs[n_in + n_out:n_in + n_out + N_SCR]
    wqf, wp, stage, stage_p, load_sem, store_sem = refs[n_in + n_out + N_SCR:]
    width = tok_ref.shape[1]
    high = wp.shape[1]
    per = width // high
    core = tab[0, 64]

    def chip_of(kind, who, slot, flip):
        return tab[0, ((kind * 2 + who) * 8 + slot) * 2 + flip]

    def rows_of(chip):
        return pl.ds(pl.multiple_of(chip * high, high), high)

    whole = {"qo": (wqf.at[0:4], 0), "f": (wqf.at[4:8], 1), "p": (wp, 2)}

    def pull(src, dst, part):
        pltpu.make_async_copy(src, dst, load_sem.at[whole[part][1]]).start()

    if fast:
        k = 0
        for who in range(2):
            c = core if who == 0 else 1 - core
            for slot in range(8):
                for flip in range(2):
                    chip = chip_of(0, who, slot, flip)
                    cols = pl.ds(2 * c, 2)
                    cols_f = pl.ds(4 + 2 * c, 2)
                    ps = pl.ds(4 * chip + 2 * c, 2)
                    if slot == 0:
                        one, two = w_in[k], w_in[k + 1]
                        k += 2
                        pull(one.at[0:2], wqf.at[cols, rows_of(chip), :], "qo")
                        pull(one.at[2], wqf.at[4 + 2 * c, rows_of(chip), :], "f")
                        pull(two.at[0], wqf.at[5 + 2 * c, rows_of(chip), :], "f")
                        pull(two.at[1:3], wp.at[ps], "p")
                    else:
                        one = w_in[k]
                        k += 1
                        pull(one.at[0:2], wqf.at[cols, rows_of(chip), :], "qo")
                        pull(one.at[2:4], wqf.at[cols_f, rows_of(chip), :], "f")
                        pull(one.at[4:6], wp.at[ps], "p")
    else:
        pull(w_in[0].at[0:4], wqf.at[0:4], "qo")
        pull(w_in[0].at[4:8], wqf.at[4:8], "f")
        pull(w_in[1], wp, "p")

    arrived = set()

    def ready(part):
        if part not in arrived:
            arrived.add(part)
            ref, s = whole[part]
            pltpu.make_async_copy(ref, ref, load_sem.at[s]).wait()

    def load_qf(k):
        return wqf[k]

    def load_p(i):
        return wp[pl.ds(i * per, per)].reshape(width, width)

    def drain(ref, s):
        pltpu.make_async_copy(ref, ref, store_sem.at[s]).wait()

    def push(src, dst, s):
        pltpu.make_async_copy(src, dst, store_sem.at[s]).start()

    part_rows = width // 2

    def product(left, right, out):
        @pl.loop(0, 2)
        def _(r):
            cols = pl.ds(pl.multiple_of(r * part_rows, part_rows), part_rows)
            value = dot(left[:, cols], right[...], TN).astype(BF16)
            out[pl.ds(r * (per // 2), per // 2)] = value.reshape(per // 2, high, width)

    def keep_refs(slot, flip):
        for i, offs in enumerate(BATCHES):
            if OFFSETS[slot] in offs:
                at = offs.index(OFFSETS[slot])
                return d_out[3 * i + flip].at[at], d_out[3 * i + 2].at[flip, at]

    def emit(a_all, att_all, c_all, ga_all, dmix_all, gb_all, dpre_all, gd_all):
        @pl.loop(0, 4)
        def _(i):
            product(ga_all.at[i], gd_all, stage_p.at[pl.ds(i * per, per)])
        if fast:
            for slot in range(8):
                for flip in range(2):
                    kept, sent = keep_refs(slot, flip)
                    for who, dst in ((0, kept), (1, sent)):
                        c = core if who == 0 else 1 - core
                        chip = chip_of(1, who, slot, flip)
                        push(stage_p.at[pl.ds(4 * chip + 2 * c, 2)], dst.at[4:6], 2)
        else:
            push(stage_p, d_out[1], 2)

        for job in range(4):
            s = job % 2
            if job >= 2:
                drain(stage.at[s], s)
            half = job % 2
            if job < 2:
                for h in range(2):
                    product(c_all, dpre_all.at[2 * half + h], stage.at[s, h])
            elif half == 0:
                for h in range(2):
                    product(a_all, dmix_all.at[h], stage.at[s, h])
            else:
                product(a_all, dmix_all.at[2], stage.at[s, 0])
                product(att_all, gb_all, stage.at[s, 1])
            g = 1 if job < 2 else 0
            if not fast:
                push(stage.at[s, 0], d_out[0].at[4 * g + 2 * half], s)
                push(stage.at[s, 1], d_out[0].at[4 * g + 2 * half + 1], s)
                continue
            for slot in range(8):
                for flip in range(2):
                    kept, sent = keep_refs(slot, flip)

                    @pl.when(core == half)
                    def _():
                        push(stage.at[s, :, chip_of(1, 0, slot, flip)], kept.at[2 * g:2 * g + 2], s)

                    @pl.when(core != half)
                    def _():
                        push(stage.at[s, :, chip_of(1, 1, slot, flip)], sent.at[2 * g:2 * g + 2], s)
        drain(stage.at[0], 0)
        drain(stage.at[1], 1)
        drain(stage_p, 2)

    compute(len_ref, tok_ref, cot_ref, sm_ref, act_ref, tg_ref, sg_ref, scr, (load_qf, load_p), ready, emit)


def run_kernel(fast, table, lengths, tokens, cotangent, smalls, w_in, d_shapes):
    rows, width = tokens.shape
    high = 48
    per = width // high
    n_in = 5 + len(w_in)
    smem = pl.BlockSpec(memory_space=pltpu.SMEM)
    vmem = pl.BlockSpec(memory_space=pltpu.VMEM)
    hbm = pl.BlockSpec(memory_space=pl.ANY)
    out_shape = [
        jax.ShapeDtypeStruct((rows, width), BF16),
        jax.ShapeDtypeStruct((rows, width), BF16),
        jax.ShapeDtypeStruct((1, 12 * width), F32),
    ] + [jax.ShapeDtypeStruct(s, BF16) for s in d_shapes]
    return pl.pallas_call(
        functools.partial(kernel, fast, n_in, len(out_shape)),
        out_shape=out_shape,
        in_specs=[smem, smem, vmem, vmem, vmem] + [hbm] * len(w_in),
        out_specs=[vmem, vmem, vmem] + [hbm] * len(d_shapes),
        scratch_shapes=compute_scratch(rows, width) + [
            pltpu.VMEM((8, width, width), BF16),
            pltpu.VMEM((4 * per, high, width), BF16),
            pltpu.VMEM((2, 2, per, high, width), BF16),
            pltpu.VMEM((4 * per, high, width), BF16),
            pltpu.SemaphoreType.DMA((3,)),
            pltpu.SemaphoreType.DMA((3,)),
        ],
        compiler_params=pltpu.CompilerParams(vmem_limit_bytes=LIMIT),
        cost_estimate=pl.CostEstimate(flops=22_000_000_000, bytes_accessed=32_000_000, transcendentals=4_000_000),
        name="blocks",
    )(table, lengths, tokens, cotangent, smalls, *w_in)


VECTORS = ("g1", "s1", "qv", "ob", "g2", "s2", "fb", "pb")


def spread(vectors, count, me):
    parts = []
    for v in vectors:
        mine = v.astype(BF16).astype(F32)
        owner = lax.broadcasted_iota(jnp.int32, (count, v.shape[0]), 0)
        parts.append(jnp.where(owner == me, mine[None, :], 0.0).reshape(-1))
    return jnp.concatenate(parts)


def own_parts(packed, sizes, count, me):
    parts, base = [], 0
    for size in sizes:
        parts.append(lax.dynamic_slice(packed, (base + me * size,), (size,)))
        base += size * count
    return parts


def total_small(packed, steps):
    for axis, pairs in steps:
        packed = packed + lax.ppermute(packed, axis, pairs)
    return packed


def swap_steps(sizes):
    steps = []
    for axis, size in sizes:
        bit = 1
        while bit < size:
            steps.append((axis, [(i, i ^ bit) for i in range(size)]))
            bit *= 2
    return steps


def gather_pieces(piece):
    cw, ccw, swap, pair = ring_pairs(1), ring_pairs(-1), swap_pairs(), core_pairs()

    def go(v, pairs):
        return lax.ppermute(v, AXES, pairs)

    got = {(0, 0): [piece]}
    right = left = piece
    newest = [((0, 0), 0)]
    for step in range(1, 5):
        if step < 4:
            right, left = go(right, cw), go(left, ccw)
            got[(step, 0)], got[(-step, 0)] = [right], [left]
            arrivals = [((step, 0), 0), ((-step, 0), 0)]
        else:
            half = piece.shape[0] // 2
            got[(4, 0)] = [go(right[:half], cw), go(left[half:], ccw)]
            got[(4, 1)] = [None, None]
            arrivals = [((4, 0), 0), ((4, 0), 1)]
        for (off, _), k in newest:
            got[(off, 1)] = [go(got[(off, 0)][k], swap)]
        newest = arrivals
    for (off, _), k in newest:
        got[(off, 1)][k] = go(got[(off, 0)][k], swap)
    own, other = [], []
    for off in OFFSETS:
        for flip in range(2):
            own += got[(off, flip)]
    other = [go(v, pair) for v in own]
    return own + other


def scatter_sums(outs):
    cw, ccw, swap, pair = ring_pairs(1), ring_pairs(-1), swap_pairs(), core_pairs()

    def go(v, pairs):
        return lax.ppermute(v, AXES, pairs)

    def add(a, b):
        return (a.astype(F32) + b.astype(F32)).astype(BF16)

    sums = []
    for i in range(len(BATCHES)):
        kept, flipped, sent = outs[3 * i:3 * i + 3]
        got = go(sent, pair)
        moved = go(add(flipped, got[1]), swap)
        sums.append((kept.astype(F32) + got[0].astype(F32) + moved.astype(F32)))
    half = sums[0].shape[1] // 2
    first = sums[0][0].astype(BF16)
    right, left = go(first[:half], cw), go(first[half:], ccw)
    zero = jnp.zeros_like(right)
    right = (sums[1][0] + jnp.concatenate([right, zero]).astype(F32)).astype(BF16)
    left = (sums[1][1] + jnp.concatenate([zero, left]).astype(F32)).astype(BF16)
    for i in (2, 3):
        right, left = go(right, cw), go(left, ccw)
        right = (sums[i][0] + right.astype(F32)).astype(BF16)
        left = (sums[i][1] + left.astype(F32)).astype(BF16)
    right, left = go(right, cw), go(left, ccw)
    return sums[4][0] + right.astype(F32) + left.astype(F32)


def body(sizes, tokens, lengths, ln1_gain, ln1_shift, w_qkv, qv_bias, w_out, out_bias, ln2_gain, ln2_shift,
         w_fc, fc_bias, w_proj, proj_bias, cotangent):
    dp, fsdp = sizes
    count = dp * fsdp
    me = lax.axis_index("dp") * fsdp + lax.axis_index("fsdp")
    bins, n, width = tokens.shape
    fast = (dp, fsdp) == (4, 8)
    vectors = (ln1_gain, ln1_shift, qv_bias, out_bias, ln2_gain, ln2_shift, fc_bias, proj_bias)
    steps = swap_steps((("fsdp", fsdp), ("dp", dp)))
    smalls = total_small(spread(vectors, count, me), steps).reshape(1, 12 * width)
    part = w_qkv.shape[0]
    wide = jnp.stack([
        w_qkv[:, :width], w_qkv[:, width:2 * width], w_qkv[:, 2 * width:], w_out,
        w_fc[:, :width], w_fc[:, width:2 * width], w_fc[:, 2 * width:3 * width], w_fc[:, 3 * width:],
    ]).astype(BF16)
    proj = w_proj.astype(BF16)
    flat = (lengths.reshape(bins, -1), tokens.reshape(-1, width), cotangent.reshape(-1, width), smalls)
    if fast:
        core = me % 2
        chips = jnp.array(TABLE, jnp.int32)
        table = lax.dynamic_slice(chips, (me, 0), (1, chips.shape[1]))
        halves = wide.reshape(2, 2, 2, part, width)
        mine = jnp.where(core == 0, halves[:, 0], halves[:, 1])
        theirs = jnp.where(core == 0, halves[:, 1], halves[:, 0])
        other = lax.ppermute(theirs, AXES, core_pairs())
        both = jnp.where(core == 0, jnp.concatenate([mine, other], 2), jnp.concatenate([other, mine], 2))
        piece = jnp.concatenate([both.reshape(4, 2 * part, width), proj.reshape(2, 2 * part, width)])
        pieces = gather_pieces(piece)
        shape = piece.shape
        d_shapes = []
        for offs in BATCHES:
            k = len(offs)
            d_shapes += [(k,) + shape, (k,) + shape, (2, k) + shape]
        act, tgrad, small_sums, *outs = run_kernel(True, table, *flat, pieces, d_shapes)
        total = scatter_sums(outs)
        high = total[:4, :part], total[:4, part:]
        own = jnp.where(core == 0, high[0], high[1])
        got = lax.ppermute(jnp.where(core == 0, high[1], high[0]), AXES, core_pairs())
        own, got = own.reshape(2, 2, part, width), got.reshape(2, 2, part, width)
        blocks = jnp.where(core == 0, jnp.concatenate([own, got], 1), jnp.concatenate([got, own], 1))
        blocks = blocks.reshape(8, part, width)
        d_proj = total[4:].reshape(w_proj.shape)
    else:
        table = jnp.zeros((1, 65), jnp.int32)
        w_all = lax.all_gather(wide, AXES, axis=1, tiled=True)
        p_all = lax.all_gather(proj, AXES, axis=0, tiled=True).reshape(-1, 48, width)
        act, tgrad, small_sums, d_wide, d_p = run_kernel(
            False, table, *flat, [w_all, p_all], [(8,) + (p_all.shape[0] // 4,) + p_all.shape[1:], p_all.shape])
        blocks = lax.psum_scatter(d_wide.reshape(w_all.shape), AXES, scatter_dimension=1, tiled=True).astype(F32)
        d_proj = lax.psum_scatter(d_p.reshape(-1, width), AXES, scatter_dimension=0, tiled=True).astype(F32)
    small = own_parts(total_small(small_sums.reshape(-1), steps), [v.shape[0] for v in vectors], count, me)
    g1, s1, qv, ob, g2, s2, fb, pb = small
    d_qkv = jnp.concatenate([blocks[0], blocks[1], blocks[2]], axis=1)
    d_fc = jnp.concatenate([blocks[4], blocks[5], blocks[6], blocks[7]], axis=1)
    return (act.reshape(tokens.shape), tgrad.reshape(tokens.shape), g1, s1, d_qkv, qv, blocks[3], ob, g2, s2,
            d_fc, fb, d_proj, pb)


def make_table():
    gather, scatter = relative_chips(-1), relative_chips(1)
    rows = []
    for chip in range(16):
        for core in range(2):
            row = []
            for table in (gather, scatter):
                for who in range(2):
                    for slot in range(8):
                        row += table[chip][core ^ who][slot]
            rows.append(row + [core])
    return rows


TABLE = make_table()


def solution(mesh):
    both = P(AXES)
    rows = P(None, AXES, None)
    matrix = P(AXES, None)
    weights = (both, both, matrix, both, matrix, both, both, both, matrix, both, matrix, both)
    return jax.shard_map(
        functools.partial(body, (mesh.shape["dp"], mesh.shape["fsdp"])),
        mesh=mesh,
        in_specs=(rows, rows) + weights + (rows,),
        out_specs=(rows, rows) + weights,
        check_vma=False,
    )
```

```python
import functools

import jax
import jax.numpy as jnp
from jax import lax
from jax.experimental import pallas as pl
from jax.experimental.pallas import tpu as pltpu
from jax.sharding import PartitionSpec as P

HEADS = 12
HD = 64
EPS = 1e-05
NEG = -1e30
AXES = ("dp", "fsdp")
F32 = jnp.float32
BF16 = jnp.bfloat16
GELU_A = 0.7978845608028654
GELU_B = 0.044715

NT = (((1,), (1,)), ((), ()))
TN = (((0,), (0,)), ((), ()))
NN = (((1,), (0,)), ((), ()))

CYCLE = [(0, 0), (0, 1), (0, 2), (0, 3), (1, 3), (1, 2), (1, 1), (1, 0)]
OFFSETS = (4, 3, -3, 2, -2, 1, -1, 0)
BATCHES = ((4,), (3, -3), (2, -2), (1, -1), (0,))


def place(core, u, o, z):
    x, y = (o, u) if core == 0 else (u, o)
    return (y * 2 + x) * 4 + z


def device_of(chip, core):
    return chip * 2 + core


def ring_pairs(step):
    pairs = []
    for core in range(2):
        for o in range(2):
            for i, (u, z) in enumerate(CYCLE):
                u2, z2 = CYCLE[(i + step) % 8]
                pairs.append((device_of(place(core, u, o, z), core), device_of(place(core, u2, o, z2), core)))
    return pairs


def swap_pairs():
    pairs = []
    for core in range(2):
        for o in range(2):
            for u, z in CYCLE:
                pairs.append((device_of(place(core, u, o, z), core), device_of(place(core, u, 1 - o, z), core)))
    return pairs


def core_pairs():
    return [(d, d ^ 1) for d in range(32)]


def relative_chips(sign):
    table = [[[[0, 0] for _ in OFFSETS] for _ in range(2)] for _ in range(16)]
    for core in range(2):
        for o in range(2):
            for i, (u, z) in enumerate(CYCLE):
                me = place(core, u, o, z)
                for slot, off in enumerate(OFFSETS):
                    u2, z2 = CYCLE[(i + sign * off) % 8]
                    for flip in range(2):
                        table[me][core][slot][flip] = place(core, u2, o ^ flip, z2)
    return table


def dot(a, b, dims):
    return lax.dot_general(a, b, dims, preferred_element_type=F32)


SMALL = dict(g1=0, s1=1, qb=2, vb=3, ob=4, g2=5, s2=6, fb=7, pb=11)

def compute(len_ref, tok_ref, cot_ref, sm_ref, act_ref, tg_ref, sg_ref, scr, loaders, ready, emit):
    wide, proj = loaders
    (a_all, att_all, c_all, ga_all, slope_all, mix_all, xh1_all, xh2_all, rs1_all, rs2_all, prob_all,
     gd_all, gb_all, dpre_all, dmix_all, hid, acc, datt) = scr
    rows, width = tok_ref.shape
    bins = len_ref.shape[0]
    n = rows // bins

    def small(name):
        return sm_ref[:, SMALL[name] * width:(SMALL[name] + 1) * width]

    def add_small(name, value):
        ks = slice(SMALL[name] * width, (SMALL[name] + 1) * width)
        sg_ref[:, ks] = sg_ref[:, ks] + value

    def fc_cols(i):
        return slice((SMALL["fb"] + i) * width, (SMALL["fb"] + i + 1) * width)

    sg_ref[...] = jnp.zeros_like(sg_ref)
    low_half = lax.broadcasted_iota(jnp.int32, (n, 2 * HD), 1) < HD
    key_i = lax.broadcasted_iota(jnp.int32, (n, n), 0)
    query_i = lax.broadcasted_iota(jnp.int32, (n, n), 1)
    allowed = []
    for m in range(bins):
        seg_k = jnp.zeros((n, n), jnp.int32)
        seg_q = jnp.zeros((n, n), jnp.int32)
        end = jnp.int32(0)
        for i in range(len_ref.shape[1]):
            end = end + len_ref[m, i]
            seg_k += (key_i >= end).astype(jnp.int32)
            seg_q += (query_i >= end).astype(jnp.int32)
        allowed.append(jnp.logical_and(seg_k == seg_q, key_i <= query_i))

    def halves(v):
        zero = jnp.zeros_like(v)
        return jnp.where(low_half, v, zero), jnp.where(low_half, zero, v)

    def fold(v):
        return jnp.sum(v.reshape(v.shape[0] // 8, 8, v.shape[1]), axis=0)

    def forward_norm(v, rs, gain, shift, dst, xh_all, rs_all):
        cen = v - jnp.mean(v, axis=-1, keepdims=True)
        rstd = lax.rsqrt(jnp.mean(cen * cen, axis=-1, keepdims=True) + EPS)
        xhat = cen * rstd
        xh_all[rs, :] = xhat
        rs_all[rs, :] = jnp.broadcast_to(rstd, (rows, 128))
        dst[rs, :] = (xhat * gain + shift).astype(BF16)

    def backward_norm(xh_all, rs_all, rs, gain, names):
        xhat = xh_all[rs, :]
        dy = acc[...]
        dx = dy * gain
        m1 = jnp.mean(dx, axis=-1, keepdims=True)
        m2 = jnp.mean(dx * xhat, axis=-1, keepdims=True)
        add_small(names[0], jnp.sum(fold(dy * xhat), axis=0, keepdims=True))
        add_small(names[1], jnp.sum(fold(dy), axis=0, keepdims=True))
        return hid[...] + rs_all[rs, 0:1] * (dx - m1 - xhat * m2)

    def colsum(v16):
        return jnp.sum(fold(v16.astype(F32)), axis=0, keepdims=True)

    def stack(v):
        return jnp.concatenate(halves(v), axis=0)

    def unstack(v):
        return jnp.where(low_half, v[:n], v[n:])

    def pairs(base, body):
        for hp in range(HEADS // 2):
            body(slice(hp * 2 * HD, (hp + 1) * 2 * HD), [slice(base + m * n, base + (m + 1) * n) for m in range(bins)], hp)

    def forward(b):
        base = b * rows
        rs = slice(base, base + rows)
        forward_norm(acc[...], rs, small("g1"), small("s1"), a_all, xh1_all, rs1_all)
        ready("qo")
        mix_all[0, rs, :] = (dot(a_all[rs, :], wide(0), NN) + small("qb")).astype(BF16)
        mix_all[1, rs, :] = dot(a_all[rs, :], wide(1), NN).astype(BF16)
        mix_all[2, rs, :] = (dot(a_all[rs, :], wide(2), NN) + small("vb")).astype(BF16)

        def head_pair(ls, rms, hp):
            scores = [dot(stack(mix_all[1, rm, ls] * (HD ** -0.5)), mix_all[0, rm, ls], NT) for rm in rms]
            probs = []
            for m, v in enumerate(scores):
                v = jnp.where(allowed[m], v.reshape(2, n, n), NEG)
                e = jnp.exp(v - jnp.max(v, axis=1, keepdims=True))
                probs.append(e * (1.0 / jnp.sum(e, axis=1, keepdims=True)))
            for m, rm in enumerate(rms):
                prob_all[(b * bins + m) * (HEADS // 2) + hp] = probs[m]
                p16 = probs[m].reshape(2 * n, n).astype(BF16)
                att_all[rm, ls] = dot(p16, stack(mix_all[2, rm, ls]), TN).astype(BF16)
        pairs(base, head_pair)

        mid = acc[...] + (dot(att_all[rs, :], wide(3), NN) + small("ob"))
        acc[...] = mid + small("pb")
        forward_norm(mid, rs, small("g2"), small("s2"), c_all, xh2_all, rs2_all)
        ready("f")
        ready("p")

        for i in range(4):
            v = dot(c_all[rs, :], wide(4 + i), NN) + sm_ref[:, fc_cols(i)]
            v2 = v * v
            t = jnp.tanh(v * (GELU_A + (GELU_A * GELU_B) * v2))
            half = 0.5 + 0.5 * t
            ga_all[i, rs, :] = (v * half).astype(BF16)
            slope_all[i, rs, :] = half * (1.0 + v * (1.0 - t) * (GELU_A + (3.0 * GELU_A * GELU_B) * v2))
            acc[...] += dot(ga_all[i, rs, :], proj(i), NN)

    def backward(b):
        base = b * rows
        rs = slice(base, base + rows)
        add_small("pb", colsum(gd_all[rs, :]))
        acc[...] = jnp.zeros_like(acc)
        for i in range(4):
            d = (dot(gd_all[rs, :], proj(i), NT) * slope_all[i, rs, :]).astype(BF16)
            dpre_all[i, rs, :] = d
            sg_ref[:, fc_cols(i)] = sg_ref[:, fc_cols(i)] + colsum(d)
            acc[...] += dot(dpre_all[i, rs, :], wide(4 + i), NT)

        dmid = backward_norm(xh2_all, rs2_all, rs, small("g2"), ("g2", "s2"))
        hid[...] = dmid
        gb_all[rs, :] = dmid.astype(BF16)
        add_small("ob", colsum(gb_all[rs, :]))
        datt[...] = dot(gb_all[rs, :], wide(3), NT).astype(BF16)

        def head_pair(ls, rms, hp):
            outs = [datt[m * n:(m + 1) * n, ls] for m in range(bins)]
            dprobs = [dot(stack(mix_all[2, rm, ls]), outs[m], NT) for m, rm in enumerate(rms)]
            for m, rm in enumerate(rms):
                p = prob_all[(b * bins + m) * (HEADS // 2) + hp]
                dmix_all[2, rm, ls] = unstack(dot(p.reshape(2 * n, n).astype(BF16), outs[m], NN)).astype(BF16)
            dscores = []
            for m in range(bins):
                p = prob_all[(b * bins + m) * (HEADS // 2) + hp]
                dp = dprobs[m].reshape(2, n, n)
                ds = p * (dp - jnp.sum(p * dp, axis=1, keepdims=True))
                dscores.append(ds.reshape(2 * n, n).astype(BF16))
            for m, rm in enumerate(rms):
                ds = dscores[m]
                dmix_all[1, rm, ls] = (unstack(dot(ds, mix_all[0, rm, ls], NN)) * (HD ** -0.5)).astype(BF16)
                dmix_all[0, rm, ls] = (dot(ds, stack(mix_all[1, rm, ls]), TN) * (HD ** -0.5)).astype(BF16)
        pairs(base, head_pair)

        add_small("qb", colsum(dmix_all[0, rs, :]))
        add_small("vb", colsum(dmix_all[2, rs, :]))
        acc[...] = dot(dmix_all[0, rs, :], wide(0), NT)
        acc[...] += dot(dmix_all[1, rs, :], wide(1), NT)
        acc[...] += dot(dmix_all[2, rs, :], wide(2), NT)
        dh = backward_norm(xh1_all, rs1_all, rs, small("g1"), ("g1", "s1"))
        hid[...] = dh
        (gd_all if b == 1 else tg_ref)[0:rows, :] = dh.astype(BF16)

    acc[...] = tok_ref[...].astype(F32)
    forward(0)
    forward(1)
    act_ref[...] = acc[...].astype(BF16)
    hid[...] = cot_ref[...].astype(F32)
    gd_all[rows:2 * rows, :] = cot_ref[...]
    backward(1)
    backward(0)
    emit(a_all, att_all, c_all, ga_all, dmix_all, gb_all, dpre_all, gd_all)


def compute_scratch(rows, width):
    two = 2 * rows
    return [
        pltpu.VMEM((two, width), BF16),
        pltpu.VMEM((two, width), BF16),
        pltpu.VMEM((two, width), BF16),
        pltpu.VMEM((4, two, width), BF16),
        pltpu.VMEM((4, two, width), F32),
        pltpu.VMEM((3, two, width), BF16),
        pltpu.VMEM((two, width), F32),
        pltpu.VMEM((two, width), F32),
        pltpu.VMEM((two, 128), F32),
        pltpu.VMEM((two, 128), F32),
        pltpu.VMEM((2 * HEADS, 2, rows // 2, rows // 2), F32),
        pltpu.VMEM((two, width), BF16),
        pltpu.VMEM((two, width), BF16),
        pltpu.VMEM((4, two, width), BF16),
        pltpu.VMEM((3, two, width), BF16),
        pltpu.VMEM((rows, width), F32),
        pltpu.VMEM((rows, width), F32),
        pltpu.VMEM((rows, width), BF16),
    ]


N_SCR = 18
LIMIT = 64 * 1024 * 1024


def kernel(fast, n_in, n_out, *refs):
    tab, len_ref, tok_ref, cot_ref, sm_ref = refs[:5]
    w_in = refs[5:n_in]
    act_ref, tg_ref, sg_ref = refs[n_in:n_in + 3]
    d_out = refs[n_in + 3:n_in + n_out]
    scr = refs[n_in + n_out:n_in + n_out + N_SCR]
    wqf, wp, load_sem, store_sem = refs[n_in + n_out + N_SCR:]
    width = tok_ref.shape[1]
    high = wp.shape[1]
    per = width // high
    core = tab[0, 64]

    def chip_of(kind, who, slot, flip):
        return tab[0, ((kind * 2 + who) * 8 + slot) * 2 + flip]

    whole = {"qo": (wqf.at[0:4], 0), "f": (wqf.at[4:8], 1), "p": (wp, 2)}

    def pull(src, dst, part):
        pltpu.make_async_copy(src, dst, load_sem.at[whole[part][1]]).start()

    if fast:
        for who in range(2):
            c = core if who == 0 else 1 - core
            for flip in range(2):
                for i, offs in enumerate(BATCHES):
                    src = w_in[(who * 2 + flip) * len(BATCHES) + i]
                    for j, off in enumerate(offs):
                        chip = chip_of(0, who, OFFSETS.index(off), flip)
                        pull(src.at[6 * j:6 * j + 2], wqf.at[pl.ds(2 * c, 2), chip], "qo")
                        pull(src.at[6 * j + 2:6 * j + 4], wqf.at[pl.ds(4 + 2 * c, 2), chip], "f")
                        pull(src.at[6 * j + 4:6 * j + 6], wp.at[pl.ds(4 * chip + 2 * c, 2)], "p")
    else:
        pull(w_in[0].at[0:4], wqf.at[0:4], "qo")
        pull(w_in[0].at[4:8], wqf.at[4:8], "f")
        pull(w_in[1], wp, "p")

    arrived = set()

    def ready(part):
        if part not in arrived:
            arrived.add(part)
            ref, s = whole[part]
            pltpu.make_async_copy(ref, ref, load_sem.at[s]).wait()

    def load_qf(k):
        return wqf[k].reshape(width, width)

    def load_p(i):
        return wp[pl.ds(i * per, per)].reshape(width, width)

    def drain(ref, s):
        pltpu.make_async_copy(ref, ref, store_sem.at[s]).wait()

    def push(src, dst, s):
        pltpu.make_async_copy(src, dst, store_sem.at[s]).start()

    def product(left, right, out):
        half = width // 2
        for r in range(2):
            value = dot(left[:, r * half:(r + 1) * half], right[...], TN).astype(BF16)
            out[r * (per // 2):(r + 1) * (per // 2)] = value.reshape(per // 2, high, width)

    def keep_refs(slot, flip):
        for i, offs in enumerate(BATCHES):
            if OFFSETS[slot] in offs:
                at = offs.index(OFFSETS[slot])
                return d_out[3 * i + flip].at[at], d_out[3 * i + 2].at[flip, at]

    def emit(a_all, att_all, c_all, ga_all, dmix_all, gb_all, dpre_all, gd_all):
        for i in range(4):
            product(ga_all.at[i], gd_all, wp.at[i * per:(i + 1) * per])
        if fast:
            for slot in range(8):
                for flip in range(2):
                    kept, sent = keep_refs(slot, flip)
                    for who, dst in ((0, kept), (1, sent)):
                        c = core if who == 0 else 1 - core
                        push(wp.at[pl.ds(4 * chip_of(1, who, slot, flip) + 2 * c, 2)], dst.at[4:6], 1)
        else:
            push(wp, d_out[1], 1)

        for part, first in ((1, 4), (0, 0)):
            for half in range(2):
                k = first + 2 * half
                for h in range(2):
                    if part == 1:
                        product(c_all, dpre_all.at[2 * half + h], wqf.at[k + h])
                    elif k + h < 3:
                        product(a_all, dmix_all.at[k + h], wqf.at[k + h])
                    else:
                        product(att_all, gb_all, wqf.at[k + h])
                if not fast:
                    push(wqf.at[k:k + 2], d_out[0].at[k:k + 2], 0)
                    continue
                for slot in range(8):
                    for flip in range(2):
                        kept, sent = keep_refs(slot, flip)

                        @pl.when(core == half)
                        def _():
                            push(wqf.at[k:k + 2, chip_of(1, 0, slot, flip)], kept.at[2 * part:2 * part + 2], 0)

                        @pl.when(core != half)
                        def _():
                            push(wqf.at[k:k + 2, chip_of(1, 1, slot, flip)], sent.at[2 * part:2 * part + 2], 0)
        drain(wqf, 0)
        drain(wp, 1)

    compute(len_ref, tok_ref, cot_ref, sm_ref, act_ref, tg_ref, sg_ref, scr, (load_qf, load_p), ready, emit)


def run_kernel(fast, table, lengths, tokens, cotangent, smalls, w_in, d_shapes):
    rows, width = tokens.shape
    high = 48
    per = width // high
    n_in = 5 + len(w_in)
    smem = pl.BlockSpec(memory_space=pltpu.SMEM)
    vmem = pl.BlockSpec(memory_space=pltpu.VMEM)
    hbm = pl.BlockSpec(memory_space=pl.ANY)
    out_shape = [
        jax.ShapeDtypeStruct((rows, width), BF16),
        jax.ShapeDtypeStruct((rows, width), BF16),
        jax.ShapeDtypeStruct((1, 12 * width), F32),
    ] + [jax.ShapeDtypeStruct(s, BF16) for s in d_shapes]
    return pl.pallas_call(
        functools.partial(kernel, fast, n_in, len(out_shape)),
        out_shape=out_shape,
        in_specs=[smem, smem, vmem, vmem, vmem] + [hbm] * len(w_in),
        out_specs=[vmem, vmem, vmem] + [hbm] * len(d_shapes),
        scratch_shapes=compute_scratch(rows, width) + [
            pltpu.VMEM((8, per, high, width), BF16),
            pltpu.VMEM((4 * per, high, width), BF16),
            pltpu.SemaphoreType.DMA((3,)),
            pltpu.SemaphoreType.DMA((2,)),
        ],
        compiler_params=pltpu.CompilerParams(vmem_limit_bytes=LIMIT),
        cost_estimate=pl.CostEstimate(flops=22_000_000_000, bytes_accessed=32_000_000, transcendentals=4_000_000),
        name="blocks",
    )(table, lengths, tokens, cotangent, smalls, *w_in)


VECTORS = ("g1", "s1", "qv", "ob", "g2", "s2", "fb", "pb")


def spread(vectors, count, me):
    parts = []
    for v in vectors:
        mine = v.astype(BF16).astype(F32)
        owner = lax.broadcasted_iota(jnp.int32, (count, v.shape[0]), 0)
        parts.append(jnp.where(owner == me, mine[None, :], 0.0).reshape(-1))
    return jnp.concatenate(parts)


def own_parts(packed, sizes, count, me):
    parts, base = [], 0
    for size in sizes:
        parts.append(lax.dynamic_slice(packed, (base + me * size,), (size,)))
        base += size * count
    return parts


def total_small(packed, steps):
    for step in steps:
        packed = add_swapped(packed, step)
    return packed


def add_swapped(packed, step):
    return packed + lax.ppermute(packed, *step)


def swap_steps(sizes):
    steps = []
    for axis, size in sizes:
        bit = 1
        while bit < size:
            steps.append((axis, [(i, i ^ bit) for i in range(size)]))
            bit *= 2
    return steps


def both_ways():
    cw, ccw, swap, pair = ring_pairs(1), ring_pairs(-1), swap_pairs(), core_pairs()
    return tuple(functools.partial(lax.ppermute, axis_name=AXES, perm=p) for p in (cw, ccw, swap, pair))


def gather_pieces(piece, packed, steps):
    cw, ccw, swap, pair = both_ways()
    stage = lax.optimization_barrier
    half = piece.shape[0] // 2

    right, left = cw(piece), ccw(piece)
    s0 = swap(piece)
    c0 = pair(piece)
    packed = add_swapped(packed, steps[0])
    right, left, c0, packed = stage((right, left, c0, packed))

    p1 = jnp.concatenate([right, left])
    right, left = cw(right), ccw(left)
    s1 = swap(p1)
    c1 = pair(p1)
    c1, packed = stage((c1, packed))
    packed = add_swapped(packed, steps[1])
    right, left, s0, c1, packed = stage((right, left, s0, c1, packed))

    p2 = jnp.concatenate([right, left])
    right, left = cw(right), ccw(left)
    s2 = swap(p2)
    cs0 = pair(s0)
    cs0, packed = stage((cs0, packed))
    packed = add_swapped(packed, steps[2])
    packed, p2 = stage((packed, p2))
    c2 = pair(p2)
    right, left, s1, c2, cs0, packed = stage((right, left, s1, c2, cs0, packed))

    p3 = jnp.concatenate([right, left])
    right, left = cw(right[:half]), ccw(left[half:])
    s3 = swap(p3)
    cs1 = pair(s1)
    cs1, packed = stage((cs1, packed))
    packed = add_swapped(packed, steps[3])
    packed, p3 = stage((packed, p3))
    c3 = pair(p3)
    right, left, s2, c3, cs1, packed = stage((right, left, s2, c3, cs1, packed))

    p4 = jnp.concatenate([right, left])
    s4 = swap(p4)
    cs2 = pair(s2)
    c4 = pair(p4)
    cs2, c4, packed = stage((cs2, c4, packed))
    packed = add_swapped(packed, steps[4])
    s3, packed, cs2, c4 = stage((s3, packed, cs2, c4))
    cs3 = pair(s3)
    cs4 = pair(s4)
    return [p4, p3, p2, p1, piece, s4, s3, s2, s1, s0, c4, c3, c2, c1, c0, cs4, cs3, cs2, cs1, cs0], packed


def scatter_sums(outs, packed, steps):
    cw, ccw, swap, pair = both_ways()
    stage = lax.optimization_barrier

    def add(a, b):
        return (a.astype(F32) + b.astype(F32)).astype(BF16)

    kept, flipped, sent = outs[0::3], outs[1::3], list(outs[2::3])
    got = [pair(sent[0]), pair(sent[1]), pair(sent[2]), None, None]
    moved = [None] * 5

    def total(i):
        return kept[i].astype(F32) + got[i][0].astype(F32) + moved[i].astype(F32)

    moved[0] = swap(add(flipped[0], got[0][1]))
    sent[3], got[0] = stage((sent[3], got[0]))
    got[3] = pair(sent[3])
    moved[1] = swap(add(flipped[1], got[1][1]))
    sent[4], got[1] = stage((sent[4], got[1]))
    got[4] = pair(sent[4])
    moved[0], got[2], got[3] = stage((moved[0], got[2], got[3]))
    first = total(0)[0].astype(BF16)
    half = first.shape[0] // 2
    right, left = cw(first[:half]), ccw(first[half:])
    moved[2] = swap(add(flipped[2], got[2][1]))
    got[4], packed = stage((got[4], packed))
    packed = add_swapped(packed, steps[0])
    zero = jnp.zeros_like(right)
    moved[1], right, left, packed = stage((moved[1], right, left, packed))
    second = total(1)
    right = cw((second[0] + jnp.concatenate([right, zero]).astype(F32)).astype(BF16))
    left = ccw((second[1] + jnp.concatenate([zero, left]).astype(F32)).astype(BF16))
    moved[3] = swap(add(flipped[3], got[3][1]))
    packed = add_swapped(packed, steps[1])
    moved[2], right, left, packed = stage((moved[2], right, left, packed))
    third = total(2)
    right = cw((third[0] + right.astype(F32)).astype(BF16))
    left = ccw((third[1] + left.astype(F32)).astype(BF16))
    moved[4] = swap(add(flipped[4], got[4][1]))
    packed = add_swapped(packed, steps[2])
    moved[3], right, left, packed = stage((moved[3], right, left, packed))
    fourth = total(3)
    right = cw((fourth[0] + right.astype(F32)).astype(BF16))
    left = ccw((fourth[1] + left.astype(F32)).astype(BF16))
    packed = add_swapped(packed, steps[3])
    moved[4], packed = stage((moved[4], packed))
    packed = add_swapped(packed, steps[4])
    return total(4)[0] + right.astype(F32) + left.astype(F32), packed


def body(sizes, tokens, lengths, ln1_gain, ln1_shift, w_qkv, qv_bias, w_out, out_bias, ln2_gain, ln2_shift,
         w_fc, fc_bias, w_proj, proj_bias, cotangent):
    dp, fsdp = sizes
    count = dp * fsdp
    me = lax.axis_index("dp") * fsdp + lax.axis_index("fsdp")
    bins, n, width = tokens.shape
    fast = (dp, fsdp) == (4, 8)
    vectors = (ln1_gain, ln1_shift, qv_bias, out_bias, ln2_gain, ln2_shift, fc_bias, proj_bias)
    steps = swap_steps((("fsdp", fsdp), ("dp", dp)))
    packed = spread(vectors, count, me)
    part = w_qkv.shape[0]
    wide = jnp.stack([
        w_qkv[:, :width], w_qkv[:, width:2 * width], w_qkv[:, 2 * width:], w_out,
        w_fc[:, :width], w_fc[:, width:2 * width], w_fc[:, 2 * width:3 * width], w_fc[:, 3 * width:],
    ]).astype(BF16)
    proj = w_proj.astype(BF16)
    flat = (lengths.reshape(bins, -1), tokens.reshape(-1, width), cotangent.reshape(-1, width))
    if fast:
        core = me % 2
        chips = jnp.array(TABLE, jnp.int32)
        table = lax.dynamic_slice(chips, (me, 0), (1, chips.shape[1]))
        halves = wide.reshape(2, 2, 2, part, width)
        mine = jnp.where(core == 0, halves[:, 0], halves[:, 1])
        theirs = jnp.where(core == 0, halves[:, 1], halves[:, 0])
        other = lax.ppermute(theirs, AXES, core_pairs())
        both = jnp.where(core == 0, jnp.concatenate([mine, other], 2), jnp.concatenate([other, mine], 2))
        piece = jnp.concatenate([both.reshape(4, 2 * part, width), proj.reshape(2, 2 * part, width)])
        pieces, packed = gather_pieces(piece, packed, steps)
        shape = piece.shape
        d_shapes = []
        for offs in BATCHES:
            k = len(offs)
            d_shapes += [(k,) + shape, (k,) + shape, (2, k) + shape]
        act, tgrad, small_sums, *outs = run_kernel(True, table, *flat, packed.reshape(1, -1), pieces, d_shapes)
        total, small_sums = scatter_sums(outs, small_sums.reshape(-1), steps)
        high = total[:4, :part], total[:4, part:]
        own = jnp.where(core == 0, high[0], high[1])
        got = lax.ppermute(jnp.where(core == 0, high[1], high[0]), AXES, core_pairs())
        own, got = own.reshape(2, 2, part, width), got.reshape(2, 2, part, width)
        blocks = jnp.where(core == 0, jnp.concatenate([own, got], 1), jnp.concatenate([got, own], 1))
        blocks = blocks.reshape(8, part, width)
        d_proj = total[4:].reshape(w_proj.shape)
    else:
        table = jnp.zeros((1, 65), jnp.int32)
        w_all = lax.all_gather(wide, AXES, axis=1, tiled=True)
        p_all = lax.all_gather(proj, AXES, axis=0, tiled=True).reshape(-1, 48, width)
        blocks_all = w_all.reshape((8, -1) + p_all.shape[1:])
        act, tgrad, small_sums, d_wide, d_p = run_kernel(
            False, table, *flat, total_small(packed, steps).reshape(1, -1), [blocks_all, p_all],
            [blocks_all.shape, p_all.shape])
        blocks = lax.psum_scatter(d_wide.reshape(w_all.shape), AXES, scatter_dimension=1, tiled=True).astype(F32)
        d_proj = lax.psum_scatter(d_p.reshape(-1, width), AXES, scatter_dimension=0, tiled=True).astype(F32)
        small_sums = total_small(small_sums.reshape(-1), steps)
    small = own_parts(small_sums, [v.shape[0] for v in vectors], count, me)
    g1, s1, qv, ob, g2, s2, fb, pb = small
    d_qkv = jnp.concatenate([blocks[0], blocks[1], blocks[2]], axis=1)
    d_fc = jnp.concatenate([blocks[4], blocks[5], blocks[6], blocks[7]], axis=1)
    return (act.reshape(tokens.shape), tgrad.reshape(tokens.shape), g1, s1, d_qkv, qv, blocks[3], ob, g2, s2,
            d_fc, fb, d_proj, pb)


def make_table():
    gather, scatter = relative_chips(-1), relative_chips(1)
    rows = []
    for chip in range(16):
        for core in range(2):
            row = []
            for table in (gather, scatter):
                for who in range(2):
                    for slot in range(8):
                        row += table[chip][core ^ who][slot]
            rows.append(row + [core])
    return rows


TABLE = make_table()


def solution(mesh):
    both = P(AXES)
    rows = P(None, AXES, None)
    matrix = P(AXES, None)
    weights = (both, both, matrix, both, matrix, both, both, both, matrix, both, matrix, both)
    return jax.shard_map(
        functools.partial(body, (mesh.shape["dp"], mesh.shape["fsdp"])),
        mesh=mesh,
        in_specs=(rows, rows) + weights + (rows,),
        out_specs=(rows, rows) + weights,
        check_vma=False,
    )
```

```python
import functools

import jax
import jax.numpy as jnp
from jax import lax
from jax.experimental import pallas as pl
from jax.experimental.pallas import tpu as pltpu
from jax.sharding import PartitionSpec as P

HEADS = 12
HD = 64
EPS = 1e-05
NEG = -1e30
AXES = ("dp", "fsdp")
F32 = jnp.float32
BF16 = jnp.bfloat16
GELU_A = 0.7978845608028654
GELU_B = 0.044715

NT = (((1,), (1,)), ((), ()))
TN = (((0,), (0,)), ((), ()))
NN = (((1,), (0,)), ((), ()))

CYCLE = [(0, 0), (0, 1), (0, 2), (0, 3), (1, 3), (1, 2), (1, 1), (1, 0)]
OFFSETS = (4, 3, -3, 2, -2, 1, -1, 0)
PIECE = 19
BATCHES = ((4,), (3, -3), (2, -2), (1, -1), (0,))


def place(core, u, o, z):
    x, y = (o, u) if core == 0 else (u, o)
    return (y * 2 + x) * 4 + z


def device_of(chip, core):
    return chip * 2 + core


def ring_pairs(step):
    pairs = []
    for core in range(2):
        for o in range(2):
            for i, (u, z) in enumerate(CYCLE):
                u2, z2 = CYCLE[(i + step) % 8]
                pairs.append((device_of(place(core, u, o, z), core), device_of(place(core, u2, o, z2), core)))
    return pairs


def swap_pairs():
    pairs = []
    for core in range(2):
        for o in range(2):
            for u, z in CYCLE:
                pairs.append((device_of(place(core, u, o, z), core), device_of(place(core, u, 1 - o, z), core)))
    return pairs


def core_pairs():
    return [(d, d ^ 1) for d in range(32)]


def relative_chips(sign):
    table = [[[[0, 0] for _ in OFFSETS] for _ in range(2)] for _ in range(16)]
    for core in range(2):
        for o in range(2):
            for i, (u, z) in enumerate(CYCLE):
                me = place(core, u, o, z)
                for slot, off in enumerate(OFFSETS):
                    u2, z2 = CYCLE[(i + sign * off) % 8]
                    for flip in range(2):
                        table[me][core][slot][flip] = place(core, u2, o ^ flip, z2)
    return table


def dot(a, b, dims):
    return lax.dot_general(a, b, dims, preferred_element_type=F32)


SMALL_ROWS = (1, 1, 2, 1, 1, 1, 4, 1)
PART = 24
SMALL = dict(g1=0, s1=1, qb=2, vb=3, ob=4, g2=5, s2=6, fb=7, pb=11)

def compute(len_ref, tok_ref, cot_ref, sm_ref, act_ref, tg_ref, sg_ref, scr, loaders, ready, emit):
    wide, proj = loaders
    (a_all, att_all, c_all, ga_all, slope_all, mix_all, xh1_all, xh2_all, rs1_all, rs2_all, prob_all,
     gd_all, gb_all, dpre_all, dmix_all, hid, acc, datt) = scr
    rows, width = tok_ref.shape
    bins = len_ref.shape[0]
    n = rows // bins

    def small(name):
        return sm_ref[:, SMALL[name] * width:(SMALL[name] + 1) * width]

    def add_small(name, value):
        ks = slice(SMALL[name] * width, (SMALL[name] + 1) * width)
        sg_ref[:, ks] = sg_ref[:, ks] + value

    def fc_cols(i):
        return slice((SMALL["fb"] + i) * width, (SMALL["fb"] + i + 1) * width)

    sg_ref[...] = jnp.zeros_like(sg_ref)
    low_half = lax.broadcasted_iota(jnp.int32, (n, 2 * HD), 1) < HD
    key_i = lax.broadcasted_iota(jnp.int32, (n, n), 0)
    query_i = lax.broadcasted_iota(jnp.int32, (n, n), 1)
    allowed = []
    for m in range(bins):
        seg_k = jnp.zeros((n, n), jnp.int32)
        seg_q = jnp.zeros((n, n), jnp.int32)
        end = jnp.int32(0)
        for i in range(len_ref.shape[1]):
            end = end + len_ref[m, i]
            seg_k += (key_i >= end).astype(jnp.int32)
            seg_q += (query_i >= end).astype(jnp.int32)
        allowed.append(jnp.logical_and(seg_k == seg_q, key_i <= query_i))

    def halves(v):
        zero = jnp.zeros_like(v)
        return jnp.where(low_half, v, zero), jnp.where(low_half, zero, v)

    def fold(v):
        return jnp.sum(v.reshape(v.shape[0] // 8, 8, v.shape[1]), axis=0)

    def forward_norm(v, rs, gain, shift, dst, xh_all, rs_all):
        cen = v - jnp.mean(v, axis=-1, keepdims=True)
        rstd = lax.rsqrt(jnp.mean(cen * cen, axis=-1, keepdims=True) + EPS)
        xhat = cen * rstd
        xh_all[rs, :] = xhat
        rs_all[rs, :] = jnp.broadcast_to(rstd, (rows, 128))
        dst[rs, :] = (xhat * gain + shift).astype(BF16)

    def backward_norm(xh_all, rs_all, rs, gain, names):
        xhat = xh_all[rs, :]
        dy = acc[...]
        dx = dy * gain
        m1 = jnp.mean(dx, axis=-1, keepdims=True)
        m2 = jnp.mean(dx * xhat, axis=-1, keepdims=True)
        add_small(names[0], jnp.sum(fold(dy * xhat), axis=0, keepdims=True))
        add_small(names[1], jnp.sum(fold(dy), axis=0, keepdims=True))
        return hid[...] + rs_all[rs, 0:1] * (dx - m1 - xhat * m2)

    def colsum(v16):
        return jnp.sum(fold(v16.astype(F32)), axis=0, keepdims=True)

    def stack(v):
        return jnp.concatenate(halves(v), axis=0)

    def unstack(v):
        return jnp.where(low_half, v[:n], v[n:])

    def pairs(base, body):
        for hp in range(HEADS // 2):
            body(slice(hp * 2 * HD, (hp + 1) * 2 * HD), [slice(base + m * n, base + (m + 1) * n) for m in range(bins)], hp)

    def forward(b):
        base = b * rows
        rs = slice(base, base + rows)
        ready("qo")
        forward_norm(acc[...], rs, small("g1"), small("s1"), a_all, xh1_all, rs1_all)
        mix_all[0, rs, :] = (dot(a_all[rs, :], wide(0), NN) + small("qb")).astype(BF16)
        mix_all[1, rs, :] = dot(a_all[rs, :], wide(1), NN).astype(BF16)
        mix_all[2, rs, :] = (dot(a_all[rs, :], wide(2), NN) + small("vb")).astype(BF16)

        def head_pair(ls, rms, hp):
            scores = [dot(stack(mix_all[1, rm, ls] * (HD ** -0.5)), mix_all[0, rm, ls], NT) for rm in rms]
            probs = []
            for m, v in enumerate(scores):
                v = jnp.where(allowed[m], v.reshape(2, n, n), NEG)
                e = jnp.exp(v - jnp.max(v, axis=1, keepdims=True))
                probs.append(e * (1.0 / jnp.sum(e, axis=1, keepdims=True)))
            for m, rm in enumerate(rms):
                prob_all[(b * bins + m) * (HEADS // 2) + hp] = probs[m]
                p16 = probs[m].reshape(2 * n, n).astype(BF16)
                att_all[rm, ls] = dot(p16, stack(mix_all[2, rm, ls]), TN).astype(BF16)
        pairs(base, head_pair)

        mid = acc[...] + (dot(att_all[rs, :], wide(3), NN) + small("ob"))
        acc[...] = mid + small("pb")
        forward_norm(mid, rs, small("g2"), small("s2"), c_all, xh2_all, rs2_all)
        ready("f")
        ready("p")

        for i in range(4):
            v = dot(c_all[rs, :], wide(4 + i), NN) + sm_ref[:, fc_cols(i)]
            v2 = v * v
            t = jnp.tanh(v * (GELU_A + (GELU_A * GELU_B) * v2))
            half = 0.5 + 0.5 * t
            ga_all[i, rs, :] = (v * half).astype(BF16)
            slope_all[i, rs, :] = half * (1.0 + v * (1.0 - t) * (GELU_A + (3.0 * GELU_A * GELU_B) * v2))
            acc[...] += dot(ga_all[i, rs, :], proj(i), NN)

    def backward(b):
        base = b * rows
        rs = slice(base, base + rows)
        add_small("pb", colsum(gd_all[rs, :]))
        acc[...] = jnp.zeros_like(acc)
        for i in range(4):
            d = (dot(gd_all[rs, :], proj(i), NT) * slope_all[i, rs, :]).astype(BF16)
            dpre_all[i, rs, :] = d
            sg_ref[:, fc_cols(i)] = sg_ref[:, fc_cols(i)] + colsum(d)
            acc[...] += dot(dpre_all[i, rs, :], wide(4 + i), NT)

        dmid = backward_norm(xh2_all, rs2_all, rs, small("g2"), ("g2", "s2"))
        hid[...] = dmid
        gb_all[rs, :] = dmid.astype(BF16)
        add_small("ob", colsum(gb_all[rs, :]))
        datt[...] = dot(gb_all[rs, :], wide(3), NT).astype(BF16)

        def head_pair(ls, rms, hp):
            outs = [datt[m * n:(m + 1) * n, ls] for m in range(bins)]
            dprobs = [dot(stack(mix_all[2, rm, ls]), outs[m], NT) for m, rm in enumerate(rms)]
            for m, rm in enumerate(rms):
                p = prob_all[(b * bins + m) * (HEADS // 2) + hp]
                dmix_all[2, rm, ls] = unstack(dot(p.reshape(2 * n, n).astype(BF16), outs[m], NN)).astype(BF16)
            dscores = []
            for m in range(bins):
                p = prob_all[(b * bins + m) * (HEADS // 2) + hp]
                dp = dprobs[m].reshape(2, n, n)
                ds = p * (dp - jnp.sum(p * dp, axis=1, keepdims=True))
                dscores.append(ds.reshape(2 * n, n).astype(BF16))
            for m, rm in enumerate(rms):
                ds = dscores[m]
                dmix_all[1, rm, ls] = (unstack(dot(ds, mix_all[0, rm, ls], NN)) * (HD ** -0.5)).astype(BF16)
                dmix_all[0, rm, ls] = (dot(ds, stack(mix_all[1, rm, ls]), TN) * (HD ** -0.5)).astype(BF16)
        pairs(base, head_pair)

        add_small("qb", colsum(dmix_all[0, rs, :]))
        add_small("vb", colsum(dmix_all[2, rs, :]))
        acc[...] = dot(dmix_all[0, rs, :], wide(0), NT)
        acc[...] += dot(dmix_all[1, rs, :], wide(1), NT)
        acc[...] += dot(dmix_all[2, rs, :], wide(2), NT)
        dh = backward_norm(xh1_all, rs1_all, rs, small("g1"), ("g1", "s1"))
        hid[...] = dh
        (gd_all if b == 1 else tg_ref)[0:rows, :] = dh.astype(BF16)

    acc[...] = tok_ref[...].astype(F32)
    forward(0)
    forward(1)
    act_ref[...] = acc[...].astype(BF16)
    hid[...] = cot_ref[...].astype(F32)
    gd_all[rows:2 * rows, :] = cot_ref[...]
    backward(1)
    backward(0)
    emit(a_all, att_all, c_all, ga_all, dmix_all, gb_all, dpre_all, gd_all)


def compute_scratch(rows, width):
    two = 2 * rows
    return [
        pltpu.VMEM((two, width), BF16),
        pltpu.VMEM((two, width), BF16),
        pltpu.VMEM((two, width), BF16),
        pltpu.VMEM((4, two, width), BF16),
        pltpu.VMEM((4, two, width), F32),
        pltpu.VMEM((3, two, width), BF16),
        pltpu.VMEM((two, width), F32),
        pltpu.VMEM((two, width), F32),
        pltpu.VMEM((two, 128), F32),
        pltpu.VMEM((two, 128), F32),
        pltpu.VMEM((2 * HEADS, 2, rows // 2, rows // 2), F32),
        pltpu.VMEM((two, width), BF16),
        pltpu.VMEM((two, width), BF16),
        pltpu.VMEM((4, two, width), BF16),
        pltpu.VMEM((3, two, width), BF16),
        pltpu.VMEM((rows, width), F32),
        pltpu.VMEM((rows, width), F32),
        pltpu.VMEM((rows, width), BF16),
    ]


N_SCR = 18
LIMIT = 64 * 1024 * 1024


def kernel(fast, n_in, n_out, *refs):
    tab, len_ref, tok_ref, cot_ref, sm_in = refs[:5]
    w_in = refs[5:n_in]
    act_ref, tg_ref, sg_ref = refs[n_in:n_in + 3]
    d_out = refs[n_in + 3:n_in + n_out]
    scr = refs[n_in + n_out:n_in + n_out + N_SCR]
    wqo, wf, wp, sm_ref, load_sem, store_sem = refs[n_in + n_out + N_SCR:]
    width = tok_ref.shape[1]
    high = wp.shape[1]
    per = width // high
    core = tab[0, 64]

    def chip_of(kind, who, slot, flip):
        return tab[0, ((kind * 2 + who) * 8 + slot) * 2 + flip]

    whole = {"qo": (wqo, 0), "f": (wf, 1), "p": (wp, 2)}

    def pull(src, dst, part):
        pltpu.make_async_copy(src, dst, load_sem.at[whole[part][1]]).start()

    def pieces():
        for who in range(2):
            c = core if who == 0 else 1 - core
            for flip in range(2):
                for i, offs in enumerate(BATCHES):
                    src = w_in[(who * 2 + flip) * len(BATCHES) + i]
                    for j, off in enumerate(offs):
                        yield c, chip_of(0, who, OFFSETS.index(off), flip), src, PIECE * j

    if fast:
        for c, chip, src, k in pieces():
            pull(src.at[k:k + 7], wqo.at[c, chip], "qo")
        for c, chip, src, k in pieces():
            pull(src.at[k + 7:k + 13], wf.at[c, chip], "f")
        for c, chip, src, k in pieces():
            pull(src.at[k + 13:k + 19], wp.at[pl.ds(12 * chip + 6 * c, 6)], "p")
    else:
        for c in range(2):
            for h in range(2):
                src = w_in[0].at[2 * c + h].reshape(16, 3, high, width)
                pull(src, wqo.at[c, :, 1 + 3 * h:4 + 3 * h], "qo")
                src = w_in[0].at[4 + 2 * c + h].reshape(16, 3, high, width)
                pull(src, wf.at[c, :, 3 * h:3 * h + 3], "f")
        pull(w_in[1], wp, "p")
        sm_ref[...] = sm_in[...]

    arrived = set()

    def ready(part):
        if part not in arrived:
            arrived.add(part)
            ref, s = whole[part]
            if part == "qo" and not fast:
                for c in range(2):
                    pltpu.make_async_copy(wqo.at[c, :, 1:7], wqo.at[c, :, 1:7], load_sem.at[s]).wait()
            else:
                pltpu.make_async_copy(ref, ref, load_sem.at[s]).wait()
            if part == "qo" and fast:
                unpack_small()

    def one_hot(v, size):
        return (lax.broadcasted_iota(jnp.int32, (size, width), 0) == sm_in[v:v + 1, :]).astype(BF16)

    def owned(v):
        return lax.broadcasted_iota(jnp.int32, (32, width), 0) == sm_in[12 + v:13 + v, :]

    def first_rows():
        line = lax.broadcasted_iota(jnp.int32, (32, 32 * high), 0)
        return (lax.broadcasted_iota(jnp.int32, (32, 32 * high), 1) == high * line).astype(BF16)

    lanes = 384

    def small_parts():
        base, v = 0, 0
        for rows in SMALL_ROWS:
            for _ in range(rows):
                yield v, base, rows * PART
                v += 1
            base += rows * PART

    def unpack_small():
        tiles = wqo[:, :, 0].reshape(32 * high, width)
        packed = dot(first_rows(), tiles[:, :lanes], NN).astype(BF16)
        for v, base, size in small_parts():
            full = jnp.where(owned(v), dot(packed[:, base:base + size], one_hot(v, size), NN), 0.0)
            sm_ref[:, v * width:(v + 1) * width] = jnp.sum(full, axis=0, keepdims=True)

    def pack_small():
        packed = jnp.zeros((32, lanes), F32)
        for v, base, size in small_parts():
            mine = jnp.where(owned(v), sg_ref[:, v * width:(v + 1) * width], 0.0).astype(BF16)
            part = dot(mine, one_hot(v, size), NT).astype(BF16)
            shift = lax.broadcasted_iota(jnp.int32, (size, lanes), 1) - lax.broadcasted_iota(jnp.int32, (size, lanes), 0)
            packed += dot(part, (shift == base).astype(BF16), NN)
        tiles = dot(first_rows(), packed.astype(BF16), TN).astype(BF16)
        wqo[:, :, 0, :, :lanes] = tiles.reshape(2, 16, high, lanes)

    def view(k):
        c, h = k % 4 // 2, k % 2
        return wqo.at[c, :, 1 + 3 * h:4 + 3 * h] if k < 4 else wf.at[c, :, 3 * h:3 * h + 3]

    def load_qf(k):
        return view(k)[...].reshape(width, width)

    def load_p(i):
        return wp[pl.ds(i * per, per)].reshape(width, width)

    def drain(ref, s):
        pltpu.make_async_copy(ref, ref, store_sem.at[s]).wait()

    def push(src, dst, s):
        pltpu.make_async_copy(src, dst, store_sem.at[s]).start()

    def product(left, right, out):
        half = width // 2
        for r in range(2):
            value = dot(left[:, r * half:(r + 1) * half], right[...], TN).astype(BF16)
            tiles = out.shape[0] // 2
            out[r * tiles:(r + 1) * tiles] = value.reshape((tiles,) + out.shape[1:])

    def keep_refs(slot, flip):
        for i, offs in enumerate(BATCHES):
            if OFFSETS[slot] in offs:
                at = offs.index(OFFSETS[slot])
                return d_out[3 * i + flip].at[at], d_out[3 * i + 2].at[flip, at]

    def half_stored(c, who, slot, flip, dst):
        @pl.when(core == (c if who == 0 else 1 - c))
        def _():
            push(wqo.at[c, chip_of(1, who, slot, flip)], dst.at[0:7], 2)

    def targets():
        for slot in range(8):
            for flip in range(2):
                for who, dst in enumerate(keep_refs(slot, flip)):
                    yield core if who == 0 else 1 - core, chip_of(1, who, slot, flip), dst

    def emit(a_all, att_all, c_all, ga_all, dmix_all, gb_all, dpre_all, gd_all):
        for i in range(4):
            product(ga_all.at[i], gd_all, wp.at[i * per:(i + 1) * per])
        if fast:
            for c, chip, dst in targets():
                push(wp.at[pl.ds(12 * chip + 6 * c, 6)], dst.at[13:19], 0)
        else:
            push(wp, d_out[1], 0)
        for i in range(4):
            product(c_all, dpre_all.at[i], view(4 + i))
        if fast:
            for c, chip, dst in targets():
                push(wf.at[c, chip], dst.at[7:13], 1)
            pack_small()
        product(att_all, gb_all, view(3))
        for i in (2, 0, 1):
            product(a_all, dmix_all.at[i], view(i))
            if fast and i != 0:
                for slot in range(8):
                    for flip in range(2):
                        for who, dst in enumerate(keep_refs(slot, flip)):
                            half_stored(1 if i == 2 else 0, who, slot, flip, dst)
        if fast:
            drain(wqo, 2)
        else:
            for k in range(8):
                push(view(k), d_out[0].at[k].reshape(16, 3, high, width), 1 if k >= 4 else 2)
            for c in range(2):
                drain(wqo.at[c, :, 1:7], 2)
        drain(wf, 1)
        drain(wp, 0)

    compute(len_ref, tok_ref, cot_ref, sm_ref, act_ref, tg_ref, sg_ref, scr, (load_qf, load_p), ready, emit)


def run_kernel(fast, table, lengths, tokens, cotangent, smalls, w_in, d_shapes):
    rows, width = tokens.shape
    high = 16
    per = width // high
    n_in = 5 + len(w_in)
    smem = pl.BlockSpec(memory_space=pltpu.SMEM)
    vmem = pl.BlockSpec(memory_space=pltpu.VMEM)
    hbm = pl.BlockSpec(memory_space=pl.ANY)
    out_shape = [
        jax.ShapeDtypeStruct((rows, width), BF16),
        jax.ShapeDtypeStruct((rows, width), BF16),
        jax.ShapeDtypeStruct((1, 12 * width), F32),
    ] + [jax.ShapeDtypeStruct(s, BF16) for s in d_shapes]
    return pl.pallas_call(
        functools.partial(kernel, fast, n_in, len(out_shape)),
        out_shape=out_shape,
        in_specs=[smem, smem, vmem, vmem, vmem] + [hbm] * len(w_in),
        out_specs=[vmem, vmem, vmem] + [hbm] * len(d_shapes),
        scratch_shapes=compute_scratch(rows, width) + [
            pltpu.VMEM((2, 16, 7, high, width), BF16),
            pltpu.VMEM((2, 16, 6, high, width), BF16),
            pltpu.VMEM((4 * per, high, width), BF16),
            pltpu.VMEM((1, 12 * width), F32),
            pltpu.SemaphoreType.DMA((3,)),
            pltpu.SemaphoreType.DMA((3,)),
        ],
        compiler_params=pltpu.CompilerParams(vmem_limit_bytes=LIMIT),
        cost_estimate=pl.CostEstimate(flops=22_000_000_000, bytes_accessed=32_000_000, transcendentals=4_000_000),
        name="blocks",
    )(table, lengths, tokens, cotangent, smalls, *w_in)


VECTORS = ("g1", "s1", "qv", "ob", "g2", "s2", "fb", "pb")


def spread(vectors, count, me):
    parts = []
    for v in vectors:
        mine = v.astype(BF16).astype(F32)
        owner = lax.broadcasted_iota(jnp.int32, (count, v.shape[0]), 0)
        parts.append(jnp.where(owner == me, mine[None, :], 0.0).reshape(-1))
    return jnp.concatenate(parts)


def own_parts(packed, sizes, count, me):
    parts, base = [], 0
    for size in sizes:
        parts.append(lax.dynamic_slice(packed, (base + me * size,), (size,)))
        base += size * count
    return parts


def total_small(packed, steps):
    for step in steps:
        packed = add_swapped(packed, step)
    return packed


def add_swapped(packed, step):
    return packed + lax.ppermute(packed, *step)


def swap_steps(sizes):
    steps = []
    for axis, size in sizes:
        bit = 1
        while bit < size:
            steps.append((axis, [(i, i ^ bit) for i in range(size)]))
            bit *= 2
    return steps


def both_ways():
    cw, ccw, swap, pair = ring_pairs(1), ring_pairs(-1), swap_pairs(), core_pairs()
    return tuple(functools.partial(lax.ppermute, axis_name=AXES, perm=p) for p in (cw, ccw, swap, pair))


def gather_pieces(piece):
    cw, ccw, swap, pair = both_ways()
    stage = lax.optimization_barrier
    half = piece.shape[0] // 2

    right, left, s0, c0 = stage((cw(piece), ccw(piece), swap(piece), pair(piece)))
    p1 = jnp.concatenate([right, left])
    s1, c1, cs0 = swap(p1), pair(p1), pair(s0)
    right, left, c1, cs0 = stage((cw(right), ccw(left), c1, cs0))
    p2 = jnp.concatenate([right, left])
    s2, c2 = swap(p2), pair(p2)
    right, left, c2, s1 = stage((cw(right), ccw(left), c2, s1))
    p3 = jnp.concatenate([right, left])
    s3, c3, cs1 = swap(p3), pair(p3), pair(s1)
    right, left, c3, cs1, s2 = stage((cw(right[:half]), ccw(left[half:]), c3, cs1, s2))
    p4 = jnp.concatenate([right, left])
    s4, c4, cs2 = swap(p4), pair(p4), pair(s2)
    s3, s4, c4, cs2 = stage((s3, s4, c4, cs2))
    cs3, cs4 = pair(s3), pair(s4)
    return [p4, p3, p2, p1, piece, s4, s3, s2, s1, s0, c4, c3, c2, c1, c0, cs4, cs3, cs2, cs1, cs0]


def scatter_sums(outs):
    cw, ccw, swap, pair = both_ways()
    stage = lax.optimization_barrier

    def add(a, b):
        return (a.astype(F32) + b.astype(F32)).astype(BF16)

    kept, flipped, sent = outs[0::3], outs[1::3], list(outs[2::3])
    got = [pair(sent[0]), pair(sent[1]), pair(sent[2]), None, None]
    moved = [None] * 5

    def total(i):
        return kept[i].astype(F32) + got[i][0].astype(F32) + moved[i].astype(F32)

    moved[0] = swap(add(flipped[0], got[0][1]))
    sent[3], got[0] = stage((sent[3], got[0]))
    got[3] = pair(sent[3])
    moved[1] = swap(add(flipped[1], got[1][1]))
    sent[4], got[1] = stage((sent[4], got[1]))
    got[4] = pair(sent[4])
    moved[0], got[2], got[3] = stage((moved[0], got[2], got[3]))
    first = total(0)[0].astype(BF16)
    half = first.shape[0] // 2
    right, left = cw(first[:half]), ccw(first[half:])
    moved[2] = swap(add(flipped[2], got[2][1]))
    moved[1], right, left = stage((moved[1], right, left))
    second = total(1)
    right, left = jnp.concatenate([right, jnp.zeros_like(left)]), jnp.concatenate([jnp.zeros_like(right), left])
    right = cw((second[0] + right.astype(F32)).astype(BF16))
    left = ccw((second[1] + left.astype(F32)).astype(BF16))
    moved[3] = swap(add(flipped[3], got[3][1]))
    moved[2], right, left = stage((moved[2], right, left))
    third = total(2)
    right = cw((third[0] + right.astype(F32)).astype(BF16))
    left = ccw((third[1] + left.astype(F32)).astype(BF16))
    moved[4] = swap(add(flipped[4], got[4][1]))
    moved[3], right, left = stage((moved[3], right, left))
    fourth = total(3)
    right = cw((fourth[0] + right.astype(F32)).astype(BF16))
    left = ccw((fourth[1] + left.astype(F32)).astype(BF16))
    return total(4)[0] + right.astype(F32) + left.astype(F32)


def body(sizes, tokens, lengths, ln1_gain, ln1_shift, w_qkv, qv_bias, w_out, out_bias, ln2_gain, ln2_shift,
         w_fc, fc_bias, w_proj, proj_bias, cotangent):
    dp, fsdp = sizes
    count = dp * fsdp
    me = lax.axis_index("dp") * fsdp + lax.axis_index("fsdp")
    bins, n, width = tokens.shape
    fast = (dp, fsdp) == (4, 8)
    vectors = (ln1_gain, ln1_shift, qv_bias, out_bias, ln2_gain, ln2_shift, fc_bias, proj_bias)
    steps = swap_steps((("fsdp", fsdp), ("dp", dp)))
    part = w_qkv.shape[0]
    wide = jnp.stack([
        w_qkv[:, :width], w_qkv[:, width:2 * width], w_qkv[:, 2 * width:], w_out,
        w_fc[:, :width], w_fc[:, width:2 * width], w_fc[:, 2 * width:3 * width], w_fc[:, 3 * width:],
    ]).astype(BF16)
    proj = w_proj.astype(BF16)
    flat = (lengths.reshape(bins, -1), tokens.reshape(-1, width), cotangent.reshape(-1, width))
    if fast:
        core = me % 2
        chips = jnp.array(TABLE, jnp.int32)
        table = lax.dynamic_slice(chips, (me, 0), (1, chips.shape[1]))
        halves = wide.reshape(2, 2, 2, part, width)
        mine = jnp.where(core == 0, halves[:, 0], halves[:, 1])
        theirs = jnp.where(core == 0, halves[:, 1], halves[:, 0])
        other = lax.ppermute(theirs, AXES, core_pairs())
        both = jnp.where(core == 0, jnp.concatenate([mine, other], 2), jnp.concatenate([other, mine], 2))
        row = jnp.concatenate(vectors).astype(BF16)
        row = jnp.pad(row[None, None, :], ((0, 0), (0, 15), (0, width - row.shape[0])))
        piece = jnp.concatenate([row, both.reshape(12, 16, width), proj.reshape(6, 16, width)])
        pieces = gather_pieces(piece)
        shape = piece.shape
        d_shapes = []
        for offs in BATCHES:
            k = len(offs)
            d_shapes += [(k,) + shape, (k,) + shape, (2, k) + shape]
        act, tgrad, _, *outs = run_kernel(True, table, *flat, small_spots(), pieces, d_shapes)
        total = scatter_sums(outs)
        square = total[1:13].reshape(4, 2 * part, width)
        high = square[:, :part], square[:, part:]
        own = jnp.where(core == 0, high[0], high[1])
        got = lax.ppermute(jnp.where(core == 0, high[1], high[0]), AXES, core_pairs())
        own, got = own.reshape(2, 2, part, width), got.reshape(2, 2, part, width)
        blocks = jnp.where(core == 0, jnp.concatenate([own, got], 1), jnp.concatenate([got, own], 1))
        blocks = blocks.reshape(8, part, width)
        d_proj = total[13:].reshape(w_proj.shape)
        small, base = [], 0
        for v in vectors:
            small.append(total[0, 0, base:base + v.shape[0]])
            base += v.shape[0]
    else:
        table = jnp.zeros((1, 65), jnp.int32)
        w_all = lax.all_gather(wide, AXES, axis=1, tiled=True)
        p_all = lax.all_gather(proj, AXES, axis=0, tiled=True).reshape(-1, 16, width)
        packed = spread(vectors, count, me)
        blocks_all = w_all.reshape((8, -1) + p_all.shape[1:])
        act, tgrad, small_sums, d_wide, d_p = run_kernel(
            False, table, *flat, total_small(packed, steps).reshape(1, -1), [blocks_all, p_all],
            [blocks_all.shape, p_all.shape])
        blocks = lax.psum_scatter(d_wide.reshape(w_all.shape), AXES, scatter_dimension=1, tiled=True).astype(F32)
        d_proj = lax.psum_scatter(d_p.reshape(-1, width), AXES, scatter_dimension=0, tiled=True).astype(F32)
        small = own_parts(total_small(small_sums.reshape(-1), steps), [v.shape[0] for v in vectors], count, me)
    g1, s1, qv, ob, g2, s2, fb, pb = small
    d_qkv = jnp.concatenate([blocks[0], blocks[1], blocks[2]], axis=1)
    d_fc = jnp.concatenate([blocks[4], blocks[5], blocks[6], blocks[7]], axis=1)
    return (act.reshape(tokens.shape), tgrad.reshape(tokens.shape), g1, s1, d_qkv, qv, blocks[3], ob, g2, s2,
            d_fc, fb, d_proj, pb)


def make_table():
    gather, scatter = relative_chips(-1), relative_chips(1)
    rows = []
    for chip in range(16):
        for core in range(2):
            row = []
            for table in (gather, scatter):
                for who in range(2):
                    for slot in range(8):
                        row += table[chip][core ^ who][slot]
            rows.append(row + [core])
    return rows


TABLE = make_table()


def small_spots():
    spots, owners = [], []
    for rows in SMALL_ROWS:
        size = rows * PART
        for r in range(rows):
            spots.append([(r * 768 + col) % size for col in range(768)])
            owners.append([(r * 768 + col) // size % 2 * 16 + (r * 768 + col) // size // 2 for col in range(768)])
    return jnp.array(spots + owners, jnp.int32)


def solution(mesh):
    both = P(AXES)
    rows = P(None, AXES, None)
    matrix = P(AXES, None)
    weights = (both, both, matrix, both, matrix, both, both, both, matrix, both, matrix, both)
    return jax.shard_map(
        functools.partial(body, (mesh.shape["dp"], mesh.shape["fsdp"])),
        mesh=mesh,
        in_specs=(rows, rows) + weights + (rows,),
        out_specs=(rows, rows) + weights,
        check_vma=False,
    )
```

```python
import functools

import jax
import jax.numpy as jnp
from jax import lax
from jax.experimental import pallas as pl
from jax.experimental.pallas import tpu as pltpu
from jax.sharding import PartitionSpec as P

HEADS = 12
HD = 64
EPS = 1e-05
NEG = -1e30
AXES = ("dp", "fsdp")
F32 = jnp.float32
BF16 = jnp.bfloat16
GELU_A = 0.7978845608028654
GELU_B = 0.044715

NT = (((1,), (1,)), ((), ()))
TN = (((0,), (0,)), ((), ()))
NN = (((1,), (0,)), ((), ()))

CYCLE = [(0, 0), (0, 1), (0, 2), (0, 3), (1, 3), (1, 2), (1, 1), (1, 0)]
OFFSETS = (4, 3, -3, 2, -2, 1, -1, 0)
PIECE = 19
BATCHES = ((4,), (3, -3), (2, -2), (1, -1), (0,))


def place(core, u, o, z):
    x, y = (o, u) if core == 0 else (u, o)
    return (y * 2 + x) * 4 + z


def device_of(chip, core):
    return chip * 2 + core


def ring_pairs(step):
    pairs = []
    for core in range(2):
        for o in range(2):
            for i, (u, z) in enumerate(CYCLE):
                u2, z2 = CYCLE[(i + step) % 8]
                pairs.append((device_of(place(core, u, o, z), core), device_of(place(core, u2, o, z2), core)))
    return pairs


def swap_pairs():
    pairs = []
    for core in range(2):
        for o in range(2):
            for u, z in CYCLE:
                pairs.append((device_of(place(core, u, o, z), core), device_of(place(core, u, 1 - o, z), core)))
    return pairs


def core_pairs():
    return [(d, d ^ 1) for d in range(32)]


def relative_chips(sign):
    table = [[[[0, 0] for _ in OFFSETS] for _ in range(2)] for _ in range(16)]
    for core in range(2):
        for o in range(2):
            for i, (u, z) in enumerate(CYCLE):
                me = place(core, u, o, z)
                for slot, off in enumerate(OFFSETS):
                    u2, z2 = CYCLE[(i + sign * off) % 8]
                    for flip in range(2):
                        table[me][core][slot][flip] = place(core, u2, o ^ flip, z2)
    return table


def dot(a, b, dims):
    return lax.dot_general(a, b, dims, preferred_element_type=F32)


SMALL_ROWS = (1, 1, 2, 1, 1, 1, 4, 1)
PART = 24
SMALL = dict(g1=0, s1=1, qb=2, vb=3, ob=4, g2=5, s2=6, fb=7, pb=11)

def compute(len_ref, tok_ref, cot_ref, sm_ref, act_ref, tg_ref, sg_ref, scr, loaders, ready, emit):
    wide, proj = loaders
    (a_all, att_all, c_all, ga_all, slope_all, mix_all, xh1_all, xh2_all, rs1_all, rs2_all, prob_all,
     gd_all, gb_all, dpre_all, dmix_all, hid, acc, datt) = scr
    rows, width = tok_ref.shape
    bins = len_ref.shape[0]
    n = rows // bins

    def small(name):
        return sm_ref[:, SMALL[name] * width:(SMALL[name] + 1) * width]

    def add_small(name, value):
        ks = slice(SMALL[name] * width, (SMALL[name] + 1) * width)
        sg_ref[:, ks] = sg_ref[:, ks] + value

    def fc_cols(i):
        return slice((SMALL["fb"] + i) * width, (SMALL["fb"] + i + 1) * width)

    sg_ref[...] = jnp.zeros_like(sg_ref)
    low_half = lax.broadcasted_iota(jnp.int32, (n, 2 * HD), 1) < HD
    key_i = lax.broadcasted_iota(jnp.int32, (n, n), 0)
    query_i = lax.broadcasted_iota(jnp.int32, (n, n), 1)
    allowed = []
    for m in range(bins):
        seg_k = jnp.zeros((n, n), jnp.int32)
        seg_q = jnp.zeros((n, n), jnp.int32)
        end = jnp.int32(0)
        for i in range(len_ref.shape[1]):
            end = end + len_ref[m, i]
            seg_k += (key_i >= end).astype(jnp.int32)
            seg_q += (query_i >= end).astype(jnp.int32)
        allowed.append(jnp.logical_and(seg_k == seg_q, key_i <= query_i))

    def halves(v):
        zero = jnp.zeros_like(v)
        return jnp.where(low_half, v, zero), jnp.where(low_half, zero, v)

    def fold(v):
        return jnp.sum(v.reshape(v.shape[0] // 8, 8, v.shape[1]), axis=0)

    def forward_norm(v, rs, names, dst, xh_all, rs_all):
        cen = v - jnp.mean(v, axis=-1, keepdims=True)
        rstd = lax.rsqrt(jnp.mean(cen * cen, axis=-1, keepdims=True) + EPS)
        xhat = cen * rstd
        xh_all[rs, :] = xhat
        rs_all[rs, :] = jnp.broadcast_to(rstd, (rows, 128))
        ready("qo")
        dst[rs, :] = (xh_all[rs, :] * small(names[0]) + small(names[1])).astype(BF16)

    def backward_norm(xh_all, rs_all, rs, gain, names):
        xhat = xh_all[rs, :]
        dy = acc[...]
        dx = dy * gain
        m1 = jnp.mean(dx, axis=-1, keepdims=True)
        m2 = jnp.mean(dx * xhat, axis=-1, keepdims=True)
        add_small(names[0], jnp.sum(fold(dy * xhat), axis=0, keepdims=True))
        add_small(names[1], jnp.sum(fold(dy), axis=0, keepdims=True))
        return hid[...] + rs_all[rs, 0:1] * (dx - m1 - xhat * m2)

    def colsum(v16):
        return jnp.sum(fold(v16.astype(F32)), axis=0, keepdims=True)

    def stack(v):
        return jnp.concatenate(halves(v), axis=0)

    def unstack(v):
        return jnp.where(low_half, v[:n], v[n:])

    def pairs(base, body):
        for hp in range(HEADS // 2):
            body(slice(hp * 2 * HD, (hp + 1) * 2 * HD), [slice(base + m * n, base + (m + 1) * n) for m in range(bins)], hp)

    def forward(b):
        base = b * rows
        rs = slice(base, base + rows)
        forward_norm(acc[...], rs, ("g1", "s1"), a_all, xh1_all, rs1_all)
        mix_all[0, rs, :] = (dot(a_all[rs, :], wide(0), NN) + small("qb")).astype(BF16)
        mix_all[1, rs, :] = dot(a_all[rs, :], wide(1), NN).astype(BF16)
        mix_all[2, rs, :] = (dot(a_all[rs, :], wide(2), NN) + small("vb")).astype(BF16)

        def head_pair(ls, rms, hp):
            scores = [dot(stack(mix_all[1, rm, ls] * (HD ** -0.5)), mix_all[0, rm, ls], NT) for rm in rms]
            probs = []
            for m, v in enumerate(scores):
                v = jnp.where(allowed[m], v.reshape(2, n, n), NEG)
                e = jnp.exp(v - jnp.max(v, axis=1, keepdims=True))
                probs.append(e * (1.0 / jnp.sum(e, axis=1, keepdims=True)))
            for m, rm in enumerate(rms):
                prob_all[(b * bins + m) * (HEADS // 2) + hp] = probs[m]
                p16 = probs[m].reshape(2 * n, n).astype(BF16)
                att_all[rm, ls] = dot(p16, stack(mix_all[2, rm, ls]), TN).astype(BF16)
        pairs(base, head_pair)

        mid = acc[...] + (dot(att_all[rs, :], wide(3), NN) + small("ob"))
        acc[...] = mid + small("pb")
        forward_norm(mid, rs, ("g2", "s2"), c_all, xh2_all, rs2_all)
        ready("f")
        ready("p")

        for i in range(4):
            v = dot(c_all[rs, :], wide(4 + i), NN) + sm_ref[:, fc_cols(i)]
            v2 = v * v
            t = jnp.tanh(v * (GELU_A + (GELU_A * GELU_B) * v2))
            half = 0.5 + 0.5 * t
            ga_all[i, rs, :] = (v * half).astype(BF16)
            slope_all[i, rs, :] = half * (1.0 + v * (1.0 - t) * (GELU_A + (3.0 * GELU_A * GELU_B) * v2))
            acc[...] += dot(ga_all[i, rs, :], proj(i), NN)

    def backward(b):
        base = b * rows
        rs = slice(base, base + rows)
        add_small("pb", colsum(gd_all[rs, :]))
        acc[...] = jnp.zeros_like(acc)
        for i in range(4):
            d = (dot(gd_all[rs, :], proj(i), NT) * slope_all[i, rs, :]).astype(BF16)
            dpre_all[i, rs, :] = d
            sg_ref[:, fc_cols(i)] = sg_ref[:, fc_cols(i)] + colsum(d)
            acc[...] += dot(dpre_all[i, rs, :], wide(4 + i), NT)

        dmid = backward_norm(xh2_all, rs2_all, rs, small("g2"), ("g2", "s2"))
        hid[...] = dmid
        gb_all[rs, :] = dmid.astype(BF16)
        add_small("ob", colsum(gb_all[rs, :]))
        datt[...] = dot(gb_all[rs, :], wide(3), NT).astype(BF16)

        def head_pair(ls, rms, hp):
            outs = [datt[m * n:(m + 1) * n, ls] for m in range(bins)]
            dprobs = [dot(stack(mix_all[2, rm, ls]), outs[m], NT) for m, rm in enumerate(rms)]
            for m, rm in enumerate(rms):
                p = prob_all[(b * bins + m) * (HEADS // 2) + hp]
                dmix_all[2, rm, ls] = unstack(dot(p.reshape(2 * n, n).astype(BF16), outs[m], NN)).astype(BF16)
            dscores = []
            for m in range(bins):
                p = prob_all[(b * bins + m) * (HEADS // 2) + hp]
                dp = dprobs[m].reshape(2, n, n)
                ds = p * (dp - jnp.sum(p * dp, axis=1, keepdims=True))
                dscores.append(ds.reshape(2 * n, n).astype(BF16))
            for m, rm in enumerate(rms):
                ds = dscores[m]
                dmix_all[1, rm, ls] = (unstack(dot(ds, mix_all[0, rm, ls], NN)) * (HD ** -0.5)).astype(BF16)
                dmix_all[0, rm, ls] = (dot(ds, stack(mix_all[1, rm, ls]), TN) * (HD ** -0.5)).astype(BF16)
        pairs(base, head_pair)

        add_small("qb", colsum(dmix_all[0, rs, :]))
        add_small("vb", colsum(dmix_all[2, rs, :]))
        acc[...] = dot(dmix_all[0, rs, :], wide(0), NT)
        acc[...] += dot(dmix_all[1, rs, :], wide(1), NT)
        acc[...] += dot(dmix_all[2, rs, :], wide(2), NT)
        dh = backward_norm(xh1_all, rs1_all, rs, small("g1"), ("g1", "s1"))
        hid[...] = dh
        (gd_all if b == 1 else tg_ref)[0:rows, :] = dh.astype(BF16)

    acc[...] = tok_ref[...].astype(F32)
    forward(0)
    forward(1)
    act_ref[...] = acc[...].astype(BF16)
    hid[...] = cot_ref[...].astype(F32)
    gd_all[rows:2 * rows, :] = cot_ref[...]
    backward(1)
    backward(0)
    emit(a_all, att_all, c_all, ga_all, dmix_all, gb_all, dpre_all, gd_all)


def compute_scratch(rows, width):
    two = 2 * rows
    return [
        pltpu.VMEM((two, width), BF16),
        pltpu.VMEM((two, width), BF16),
        pltpu.VMEM((two, width), BF16),
        pltpu.VMEM((4, two, width), BF16),
        pltpu.VMEM((4, two, width), F32),
        pltpu.VMEM((3, two, width), BF16),
        pltpu.VMEM((two, width), F32),
        pltpu.VMEM((two, width), F32),
        pltpu.VMEM((two, 128), F32),
        pltpu.VMEM((two, 128), F32),
        pltpu.VMEM((2 * HEADS, 2, rows // 2, rows // 2), F32),
        pltpu.VMEM((two, width), BF16),
        pltpu.VMEM((two, width), BF16),
        pltpu.VMEM((4, two, width), BF16),
        pltpu.VMEM((3, two, width), BF16),
        pltpu.VMEM((rows, width), F32),
        pltpu.VMEM((rows, width), F32),
        pltpu.VMEM((rows, width), BF16),
    ]


N_SCR = 18
LIMIT = 64 * 1024 * 1024


def kernel(fast, n_in, n_out, *refs):
    tab, len_ref, tok_ref, cot_ref, sm_in = refs[:5]
    w_in = refs[5:n_in]
    act_ref, tg_ref, sg_ref = refs[n_in:n_in + 3]
    d_out = refs[n_in + 3:n_in + n_out]
    scr = refs[n_in + n_out:n_in + n_out + N_SCR]
    wqo, wf, wp, sm_ref, load_sem, store_sem = refs[n_in + n_out + N_SCR:]
    width = tok_ref.shape[1]
    high = wp.shape[1]
    per = width // high
    core = tab[0, 64]

    def chip_of(kind, who, slot, flip):
        return tab[0, ((kind * 2 + who) * 8 + slot) * 2 + flip]

    whole = {"qo": (wqo, 0), "f": (wf, 1), "p": (wp, 2)}

    def pull(src, dst, part):
        pltpu.make_async_copy(src, dst, load_sem.at[whole[part][1]]).start()

    def pieces():
        for who in range(2):
            c = core if who == 0 else 1 - core
            for flip in range(2):
                for i, offs in enumerate(BATCHES):
                    src = w_in[(who * 2 + flip) * len(BATCHES) + i]
                    for j, off in enumerate(offs):
                        yield c, chip_of(0, who, OFFSETS.index(off), flip), src, PIECE * j

    def pull_first():
        if fast:
            for c, chip, src, k in pieces():
                pull(src.at[k:k + 7], wqo.at[c, chip], "qo")
            return
        sm_ref[...] = sm_in[...]
        for c in range(2):
            for h in range(2):
                src = w_in[0].at[2 * c + h].reshape(16, 3, high, width)
                pull(src, wqo.at[c, :, 1 + 3 * h:4 + 3 * h], "qo")

    def pull_rest():
        if fast:
            for c, chip, src, k in pieces():
                pull(src.at[k + 7:k + 13], wf.at[c, chip], "f")
            for c, chip, src, k in pieces():
                pull(src.at[k + 13:k + 19], wp.at[pl.ds(12 * chip + 6 * c, 6)], "p")
            return
        for c in range(2):
            for h in range(2):
                src = w_in[0].at[4 + 2 * c + h].reshape(16, 3, high, width)
                pull(src, wf.at[c, :, 3 * h:3 * h + 3], "f")
        pull(w_in[1], wp, "p")

    pull_first()
    arrived = set()

    def ready(part):
        if part not in arrived:
            arrived.add(part)
            ref, s = whole[part]
            if part == "qo" and not fast:
                for c in range(2):
                    pltpu.make_async_copy(wqo.at[c, :, 1:7], wqo.at[c, :, 1:7], load_sem.at[s]).wait()
            else:
                pltpu.make_async_copy(ref, ref, load_sem.at[s]).wait()
            if part == "qo":
                pull_rest()
                if fast:
                    unpack_small()

    def one_hot(v, size):
        return (lax.broadcasted_iota(jnp.int32, (size, width), 0) == sm_in[v:v + 1, :]).astype(BF16)

    def owned(v):
        return lax.broadcasted_iota(jnp.int32, (32, width), 0) == sm_in[12 + v:13 + v, :]

    def first_rows():
        line = lax.broadcasted_iota(jnp.int32, (32, 32 * high), 0)
        return (lax.broadcasted_iota(jnp.int32, (32, 32 * high), 1) == high * line).astype(BF16)

    lanes = 384

    def small_parts():
        base, v = 0, 0
        for rows in SMALL_ROWS:
            for _ in range(rows):
                yield v, base, rows * PART
                v += 1
            base += rows * PART

    def unpack_small():
        tiles = wqo[:, :, 0].reshape(32 * high, width)
        packed = dot(first_rows(), tiles[:, :lanes], NN).astype(BF16)
        for v, base, size in small_parts():
            full = jnp.where(owned(v), dot(packed[:, base:base + size], one_hot(v, size), NN), 0.0)
            sm_ref[:, v * width:(v + 1) * width] = jnp.sum(full, axis=0, keepdims=True)

    def pack_small():
        packed = jnp.zeros((32, lanes), F32)
        for v, base, size in small_parts():
            mine = jnp.where(owned(v), sg_ref[:, v * width:(v + 1) * width], 0.0).astype(BF16)
            part = dot(mine, one_hot(v, size), NT).astype(BF16)
            shift = lax.broadcasted_iota(jnp.int32, (size, lanes), 1) - lax.broadcasted_iota(jnp.int32, (size, lanes), 0)
            packed += dot(part, (shift == base).astype(BF16), NN)
        tiles = dot(first_rows(), packed.astype(BF16), TN).astype(BF16)
        wqo[:, :, 0, :, :lanes] = tiles.reshape(2, 16, high, lanes)

    def view(k):
        c, h = k % 4 // 2, k % 2
        return wqo.at[c, :, 1 + 3 * h:4 + 3 * h] if k < 4 else wf.at[c, :, 3 * h:3 * h + 3]

    def load_qf(k):
        return view(k)[...].reshape(width, width)

    def load_p(i):
        return wp[pl.ds(i * per, per)].reshape(width, width)

    def drain(ref, s):
        pltpu.make_async_copy(ref, ref, store_sem.at[s]).wait()

    def push(src, dst, s):
        pltpu.make_async_copy(src, dst, store_sem.at[s]).start()

    def product(left, right, out):
        half = width // 2
        for r in range(2):
            value = dot(left[:, r * half:(r + 1) * half], right[...], TN).astype(BF16)
            tiles = out.shape[0] // 2
            out[r * tiles:(r + 1) * tiles] = value.reshape((tiles,) + out.shape[1:])

    def keep_refs(slot, flip):
        for i, offs in enumerate(BATCHES):
            if OFFSETS[slot] in offs:
                at = offs.index(OFFSETS[slot])
                return d_out[3 * i + flip].at[at], d_out[3 * i + 2].at[flip, at]

    def half_stored(c, who, slot, flip, dst):
        @pl.when(core == (c if who == 0 else 1 - c))
        def _():
            push(wqo.at[c, chip_of(1, who, slot, flip)], dst.at[0:7], 2)

    def targets():
        for slot in range(8):
            for flip in range(2):
                for who, dst in enumerate(keep_refs(slot, flip)):
                    yield core if who == 0 else 1 - core, chip_of(1, who, slot, flip), dst

    def emit(a_all, att_all, c_all, ga_all, dmix_all, gb_all, dpre_all, gd_all):
        for i in range(4):
            product(ga_all.at[i], gd_all, wp.at[i * per:(i + 1) * per])
        if fast:
            for c, chip, dst in targets():
                push(wp.at[pl.ds(12 * chip + 6 * c, 6)], dst.at[13:19], 0)
        else:
            push(wp, d_out[1], 0)
        for i in range(4):
            product(c_all, dpre_all.at[i], view(4 + i))
        if fast:
            for c, chip, dst in targets():
                push(wf.at[c, chip], dst.at[7:13], 1)
            pack_small()
        product(att_all, gb_all, view(3))
        for i in (2, 0, 1):
            product(a_all, dmix_all.at[i], view(i))
            if fast and i != 0:
                for slot in range(8):
                    for flip in range(2):
                        for who, dst in enumerate(keep_refs(slot, flip)):
                            half_stored(1 if i == 2 else 0, who, slot, flip, dst)
        if fast:
            drain(wqo, 2)
        else:
            for k in range(8):
                push(view(k), d_out[0].at[k].reshape(16, 3, high, width), 1 if k >= 4 else 2)
            for c in range(2):
                drain(wqo.at[c, :, 1:7], 2)
        drain(wf, 1)
        drain(wp, 0)

    compute(len_ref, tok_ref, cot_ref, sm_ref, act_ref, tg_ref, sg_ref, scr, (load_qf, load_p), ready, emit)


def run_kernel(fast, table, lengths, tokens, cotangent, smalls, w_in, d_shapes):
    rows, width = tokens.shape
    high = 16
    per = width // high
    n_in = 5 + len(w_in)
    smem = pl.BlockSpec(memory_space=pltpu.SMEM)
    vmem = pl.BlockSpec(memory_space=pltpu.VMEM)
    hbm = pl.BlockSpec(memory_space=pl.ANY)
    out_shape = [
        jax.ShapeDtypeStruct((rows, width), BF16),
        jax.ShapeDtypeStruct((rows, width), BF16),
        jax.ShapeDtypeStruct((1, 12 * width), F32),
    ] + [jax.ShapeDtypeStruct(s, BF16) for s in d_shapes]
    return pl.pallas_call(
        functools.partial(kernel, fast, n_in, len(out_shape)),
        out_shape=out_shape,
        in_specs=[smem, smem, vmem, vmem, vmem] + [hbm] * len(w_in),
        out_specs=[vmem, vmem, vmem] + [hbm] * len(d_shapes),
        scratch_shapes=compute_scratch(rows, width) + [
            pltpu.VMEM((2, 16, 7, high, width), BF16),
            pltpu.VMEM((2, 16, 6, high, width), BF16),
            pltpu.VMEM((4 * per, high, width), BF16),
            pltpu.VMEM((1, 12 * width), F32),
            pltpu.SemaphoreType.DMA((3,)),
            pltpu.SemaphoreType.DMA((3,)),
        ],
        compiler_params=pltpu.CompilerParams(vmem_limit_bytes=LIMIT),
        cost_estimate=pl.CostEstimate(flops=22_000_000_000, bytes_accessed=32_000_000, transcendentals=4_000_000),
        name="blocks",
    )(table, lengths, tokens, cotangent, smalls, *w_in)


VECTORS = ("g1", "s1", "qv", "ob", "g2", "s2", "fb", "pb")


def spread(vectors, count, me):
    parts = []
    for v in vectors:
        mine = v.astype(BF16).astype(F32)
        owner = lax.broadcasted_iota(jnp.int32, (count, v.shape[0]), 0)
        parts.append(jnp.where(owner == me, mine[None, :], 0.0).reshape(-1))
    return jnp.concatenate(parts)


def own_parts(packed, sizes, count, me):
    parts, base = [], 0
    for size in sizes:
        parts.append(lax.dynamic_slice(packed, (base + me * size,), (size,)))
        base += size * count
    return parts


def total_small(packed, steps):
    for step in steps:
        packed = add_swapped(packed, step)
    return packed


def add_swapped(packed, step):
    return packed + lax.ppermute(packed, *step)


def swap_steps(sizes):
    steps = []
    for axis, size in sizes:
        bit = 1
        while bit < size:
            steps.append((axis, [(i, i ^ bit) for i in range(size)]))
            bit *= 2
    return steps


def both_ways():
    cw, ccw, swap, pair = ring_pairs(1), ring_pairs(-1), swap_pairs(), core_pairs()
    return tuple(functools.partial(lax.ppermute, axis_name=AXES, perm=p) for p in (cw, ccw, swap, pair))


PLAN = (
    ("s0", 0, 0),
    ("s1", 1, 2),
    ("s2", 2, 4),
    ("s3", 3, 4),
    ("s4", 4, 4),
    ("c0", 1, 1),
    ("c1", 2, 2),
    ("c2", 4, 4),
    ("c3", 4, 4),
    ("c4", 4, 4),
    ("cs0", 2, 2),
    ("cs1", 3, 3),
    ("cs2", 3, 4),
    ("cs3", 4, 5),
    ("cs4", 5, 5),
)


def gather_pieces(piece, table):
    cw, ccw, swap, pair = both_ways()
    half = piece.shape[0] // 2
    have = {"p0": piece}
    right = left = piece
    for stage in range(6):
        arrivals = {}
        if stage < 4:
            if stage == 3:
                right, left = right[:half], left[half:]
            arrivals = {"right": cw(right), "left": ccw(left)}
        for what, first, _ in PLAN:
            if first == stage:
                have[what] = swap(have["p" + what[1:]]) if what[0] == "s" else pair(have[what[1:] if what[1] == "s" else "p" + what[1:]])
        if stage == 5:
            break
        arrivals |= {what: have[what] for what, _, last in PLAN if last == stage}
        if stage == 4:
            arrivals["table"] = table
        have |= dict(zip(arrivals, lax.optimization_barrier(tuple(arrivals.values()))))
        if stage < 4:
            right, left = have["right"], have["left"]
            have[f"p{stage + 1}"] = jnp.concatenate([right, left])
    return [have[f"{kind}{k}"] for kind in ("p", "s", "c", "cs") for k in (4, 3, 2, 1, 0)], have["table"]


def scatter_sums(outs):
    cw, ccw, swap, pair = both_ways()
    stage = lax.optimization_barrier

    def add(a, b):
        return (a.astype(F32) + b.astype(F32)).astype(BF16)

    kept, flipped, sent = outs[0::3], outs[1::3], list(outs[2::3])
    got = [pair(sent[0]), pair(sent[1]), pair(sent[2]), None, None]
    moved = [None] * 5

    def total(i):
        return kept[i].astype(F32) + got[i][0].astype(F32) + moved[i].astype(F32)

    moved[0] = swap(add(flipped[0], got[0][1]))
    sent[3], got[0] = stage((sent[3], got[0]))
    got[3] = pair(sent[3])
    moved[1] = swap(add(flipped[1], got[1][1]))
    sent[4], got[1] = stage((sent[4], got[1]))
    got[4] = pair(sent[4])
    moved[0], got[2], got[3] = stage((moved[0], got[2], got[3]))
    first = total(0)[0].astype(BF16)
    half = first.shape[0] // 2
    right, left = cw(first[:half]), ccw(first[half:])
    moved[2] = swap(add(flipped[2], got[2][1]))
    moved[1], right, left = stage((moved[1], right, left))
    second = total(1)
    right, left = jnp.concatenate([right, jnp.zeros_like(left)]), jnp.concatenate([jnp.zeros_like(right), left])
    right = cw((second[0] + right.astype(F32)).astype(BF16))
    left = ccw((second[1] + left.astype(F32)).astype(BF16))
    moved[3] = swap(add(flipped[3], got[3][1]))
    moved[2], right, left = stage((moved[2], right, left))
    third = total(2)
    right = cw((third[0] + right.astype(F32)).astype(BF16))
    left = ccw((third[1] + left.astype(F32)).astype(BF16))
    moved[4] = swap(add(flipped[4], got[4][1]))
    moved[3], right, left = stage((moved[3], right, left))
    fourth = total(3)
    right = cw((fourth[0] + right.astype(F32)).astype(BF16))
    left = ccw((fourth[1] + left.astype(F32)).astype(BF16))
    return total(4)[0] + right.astype(F32) + left.astype(F32)


def body(sizes, tokens, lengths, ln1_gain, ln1_shift, w_qkv, qv_bias, w_out, out_bias, ln2_gain, ln2_shift,
         w_fc, fc_bias, w_proj, proj_bias, cotangent):
    dp, fsdp = sizes
    count = dp * fsdp
    me = lax.axis_index("dp") * fsdp + lax.axis_index("fsdp")
    bins, n, width = tokens.shape
    fast = (dp, fsdp) == (4, 8)
    vectors = (ln1_gain, ln1_shift, qv_bias, out_bias, ln2_gain, ln2_shift, fc_bias, proj_bias)
    steps = swap_steps((("fsdp", fsdp), ("dp", dp)))
    part = w_qkv.shape[0]
    wide = jnp.stack([
        w_qkv[:, :width], w_qkv[:, width:2 * width], w_qkv[:, 2 * width:], w_out,
        w_fc[:, :width], w_fc[:, width:2 * width], w_fc[:, 2 * width:3 * width], w_fc[:, 3 * width:],
    ]).astype(BF16)
    proj = w_proj.astype(BF16)
    flat = (lengths.reshape(bins, -1), tokens.reshape(-1, width), cotangent.reshape(-1, width))
    if fast:
        core = me % 2
        chips = jnp.array(TABLE, jnp.int32)
        table = lax.dynamic_slice(chips, (me, 0), (1, chips.shape[1]))
        halves = wide.reshape(2, 2, 2, part, width)
        mine = jnp.where(core == 0, halves[:, 0], halves[:, 1])
        theirs = jnp.where(core == 0, halves[:, 1], halves[:, 0])
        other = lax.ppermute(theirs, AXES, core_pairs())
        both = jnp.where(core == 0, jnp.concatenate([mine, other], 2), jnp.concatenate([other, mine], 2))
        row = jnp.concatenate(vectors).astype(BF16)
        row = jnp.pad(row[None, None, :], ((0, 0), (0, 15), (0, width - row.shape[0])))
        piece = jnp.concatenate([row, both.reshape(12, 16, width), proj.reshape(6, 16, width)])
        pieces, table = gather_pieces(piece, table)
        shape = piece.shape
        d_shapes = []
        for offs in BATCHES:
            k = len(offs)
            d_shapes += [(k,) + shape, (k,) + shape, (2, k) + shape]
        act, tgrad, _, *outs = run_kernel(True, table, *flat, small_spots(), pieces, d_shapes)
        total = scatter_sums(outs)
        square = total[1:13].reshape(4, 2 * part, width)
        high = square[:, :part], square[:, part:]
        own = jnp.where(core == 0, high[0], high[1])
        got = lax.ppermute(jnp.where(core == 0, high[1], high[0]), AXES, core_pairs())
        own, got = own.reshape(2, 2, part, width), got.reshape(2, 2, part, width)
        blocks = jnp.where(core == 0, jnp.concatenate([own, got], 1), jnp.concatenate([got, own], 1))
        blocks = blocks.reshape(8, part, width)
        d_proj = total[13:].reshape(w_proj.shape)
        small, base = [], 0
        for v in vectors:
            small.append(total[0, 0, base:base + v.shape[0]])
            base += v.shape[0]
    else:
        table = jnp.zeros((1, 65), jnp.int32)
        w_all = lax.all_gather(wide, AXES, axis=1, tiled=True)
        p_all = lax.all_gather(proj, AXES, axis=0, tiled=True).reshape(-1, 16, width)
        packed = spread(vectors, count, me)
        blocks_all = w_all.reshape((8, -1) + p_all.shape[1:])
        act, tgrad, small_sums, d_wide, d_p = run_kernel(
            False, table, *flat, total_small(packed, steps).reshape(1, -1), [blocks_all, p_all],
            [blocks_all.shape, p_all.shape])
        blocks = lax.psum_scatter(d_wide.reshape(w_all.shape), AXES, scatter_dimension=1, tiled=True).astype(F32)
        d_proj = lax.psum_scatter(d_p.reshape(-1, width), AXES, scatter_dimension=0, tiled=True).astype(F32)
        small = own_parts(total_small(small_sums.reshape(-1), steps), [v.shape[0] for v in vectors], count, me)
    g1, s1, qv, ob, g2, s2, fb, pb = small
    d_qkv = jnp.concatenate([blocks[0], blocks[1], blocks[2]], axis=1)
    d_fc = jnp.concatenate([blocks[4], blocks[5], blocks[6], blocks[7]], axis=1)
    return (act.reshape(tokens.shape), tgrad.reshape(tokens.shape), g1, s1, d_qkv, qv, blocks[3], ob, g2, s2,
            d_fc, fb, d_proj, pb)


def make_table():
    gather, scatter = relative_chips(-1), relative_chips(1)
    rows = []
    for chip in range(16):
        for core in range(2):
            row = []
            for table in (gather, scatter):
                for who in range(2):
                    for slot in range(8):
                        row += table[chip][core ^ who][slot]
            rows.append(row + [core])
    return rows


TABLE = make_table()


def small_spots():
    spots, owners = [], []
    for rows in SMALL_ROWS:
        size = rows * PART
        for r in range(rows):
            spots.append([(r * 768 + col) % size for col in range(768)])
            owners.append([(r * 768 + col) // size % 2 * 16 + (r * 768 + col) // size // 2 for col in range(768)])
    return jnp.array(spots + owners, jnp.int32)


def solution(mesh):
    both = P(AXES)
    rows = P(None, AXES, None)
    matrix = P(AXES, None)
    weights = (both, both, matrix, both, matrix, both, both, both, matrix, both, matrix, both)
    return jax.shard_map(
        functools.partial(body, (mesh.shape["dp"], mesh.shape["fsdp"])),
        mesh=mesh,
        in_specs=(rows, rows) + weights + (rows,),
        out_specs=(rows, rows) + weights,
        check_vma=False,
    )
```

```python
import functools

import jax
import jax.numpy as jnp
from jax import lax
from jax.experimental import pallas as pl
from jax.experimental.pallas import tpu as pltpu
from jax.sharding import PartitionSpec as P

HEADS = 12
HD = 64
EPS = 1e-05
NEG = -1e30
AXES = ("dp", "fsdp")
F32 = jnp.float32
BF16 = jnp.bfloat16
GELU_A = 0.7978845608028654
GELU_B = 0.044715

NT = (((1,), (1,)), ((), ()))
TN = (((0,), (0,)), ((), ()))
NN = (((1,), (0,)), ((), ()))

CYCLE = [(0, 0), (0, 1), (0, 2), (0, 3), (1, 3), (1, 2), (1, 1), (1, 0)]
OFFSETS = (4, 3, -3, 2, -2, 1, -1, 0)
PIECE = 19
BATCHES = ((4,), (3, -3), (2, -2), (1, -1), (0,))


def place(core, u, o, z):
    x, y = (o, u) if core == 0 else (u, o)
    return (y * 2 + x) * 4 + z


def device_of(chip, core):
    return chip * 2 + core


def ring_pairs(step):
    pairs = []
    for core in range(2):
        for o in range(2):
            for i, (u, z) in enumerate(CYCLE):
                u2, z2 = CYCLE[(i + step) % 8]
                pairs.append((device_of(place(core, u, o, z), core), device_of(place(core, u2, o, z2), core)))
    return pairs


def swap_pairs():
    pairs = []
    for core in range(2):
        for o in range(2):
            for u, z in CYCLE:
                pairs.append((device_of(place(core, u, o, z), core), device_of(place(core, u, 1 - o, z), core)))
    return pairs


def core_pairs():
    return [(d, d ^ 1) for d in range(32)]


def relative_chips(sign):
    table = [[[[0, 0] for _ in OFFSETS] for _ in range(2)] for _ in range(16)]
    for core in range(2):
        for o in range(2):
            for i, (u, z) in enumerate(CYCLE):
                me = place(core, u, o, z)
                for slot, off in enumerate(OFFSETS):
                    u2, z2 = CYCLE[(i + sign * off) % 8]
                    for flip in range(2):
                        table[me][core][slot][flip] = place(core, u2, o ^ flip, z2)
    return table


def dot(a, b, dims):
    return lax.dot_general(a, b, dims, preferred_element_type=F32)


SMALL_ROWS = (1, 1, 2, 1, 1, 1, 4, 1)
PART = 24
SMALL = dict(g1=0, s1=1, qb=2, vb=3, ob=4, g2=5, s2=6, fb=7, pb=11)

def compute(len_ref, tok_ref, cot_ref, sm_ref, act_ref, tg_ref, sg_ref, scr, loaders, ready, emit):
    wide, proj = loaders
    (a_all, att_all, c_all, ga_all, slope_all, mix_all, xh1_all, xh2_all, rs1_all, rs2_all, prob_all,
     gd_all, gb_all, dpre_all, dmix_all, hid, acc, datt) = scr
    rows, width = tok_ref.shape
    bins = len_ref.shape[0]
    n = rows // bins

    def small(name):
        return sm_ref[:, SMALL[name] * width:(SMALL[name] + 1) * width]

    def add_small(name, value):
        ks = slice(SMALL[name] * width, (SMALL[name] + 1) * width)
        sg_ref[:, ks] = sg_ref[:, ks] + value

    def fc_cols(i):
        return slice((SMALL["fb"] + i) * width, (SMALL["fb"] + i + 1) * width)

    sg_ref[...] = jnp.zeros_like(sg_ref)
    low_half = lax.broadcasted_iota(jnp.int32, (n, 2 * HD), 1) < HD
    key_i = lax.broadcasted_iota(jnp.int32, (n, n), 0)
    query_i = lax.broadcasted_iota(jnp.int32, (n, n), 1)
    allowed = []
    for m in range(bins):
        seg_k = jnp.zeros((n, n), jnp.int32)
        seg_q = jnp.zeros((n, n), jnp.int32)
        end = jnp.int32(0)
        for i in range(len_ref.shape[1]):
            end = end + len_ref[m, i]
            seg_k += (key_i >= end).astype(jnp.int32)
            seg_q += (query_i >= end).astype(jnp.int32)
        allowed.append(jnp.logical_and(seg_k == seg_q, key_i <= query_i))

    def halves(v):
        zero = jnp.zeros_like(v)
        return jnp.where(low_half, v, zero), jnp.where(low_half, zero, v)

    def fold(v):
        return jnp.sum(v.reshape(v.shape[0] // 8, 8, v.shape[1]), axis=0)

    def forward_norm(v, rs, names, dst, xh_all, rs_all):
        cen = v - jnp.mean(v, axis=-1, keepdims=True)
        rstd = lax.rsqrt(jnp.mean(cen * cen, axis=-1, keepdims=True) + EPS)
        xhat = cen * rstd
        xh_all[rs, :] = xhat
        rs_all[rs, :] = jnp.broadcast_to(rstd, (rows, 128))
        ready("qo")
        dst[rs, :] = (xh_all[rs, :] * small(names[0]) + small(names[1])).astype(BF16)

    def backward_norm(xh_all, rs_all, rs, gain, names):
        xhat = xh_all[rs, :]
        dy = acc[...]
        dx = dy * gain
        m1 = jnp.mean(dx, axis=-1, keepdims=True)
        m2 = jnp.mean(dx * xhat, axis=-1, keepdims=True)
        add_small(names[0], jnp.sum(fold(dy * xhat), axis=0, keepdims=True))
        add_small(names[1], jnp.sum(fold(dy), axis=0, keepdims=True))
        return hid[...] + rs_all[rs, 0:1] * (dx - m1 - xhat * m2)

    def colsum(v16):
        return jnp.sum(fold(v16.astype(F32)), axis=0, keepdims=True)

    def stack(v):
        return jnp.concatenate(halves(v), axis=0)

    def unstack(v):
        return jnp.where(low_half, v[:n], v[n:])

    def pairs(base, body):
        for hp in range(HEADS // 2):
            body(slice(hp * 2 * HD, (hp + 1) * 2 * HD), [slice(base + m * n, base + (m + 1) * n) for m in range(bins)], hp)

    def forward(b):
        base = b * rows
        rs = slice(base, base + rows)
        forward_norm(acc[...], rs, ("g1", "s1"), a_all, xh1_all, rs1_all)
        mix_all[0, rs, :] = (dot(a_all[rs, :], wide(0), NN) + small("qb")).astype(BF16)
        mix_all[1, rs, :] = dot(a_all[rs, :], wide(1), NN).astype(BF16)
        mix_all[2, rs, :] = (dot(a_all[rs, :], wide(2), NN) + small("vb")).astype(BF16)

        def head_pair(ls, rms, hp):
            scores = [dot(stack(mix_all[1, rm, ls] * (HD ** -0.5)), mix_all[0, rm, ls], NT) for rm in rms]
            probs = []
            for m, v in enumerate(scores):
                v = jnp.where(allowed[m], v.reshape(2, n, n), NEG)
                e = jnp.exp(v - jnp.max(v, axis=1, keepdims=True))
                probs.append(e * (1.0 / jnp.sum(e, axis=1, keepdims=True)))
            for m, rm in enumerate(rms):
                prob_all[(b * bins + m) * (HEADS // 2) + hp] = probs[m]
                p16 = probs[m].reshape(2 * n, n).astype(BF16)
                att_all[rm, ls] = dot(p16, stack(mix_all[2, rm, ls]), TN).astype(BF16)
        pairs(base, head_pair)

        mid = acc[...] + (dot(att_all[rs, :], wide(3), NN) + small("ob"))
        acc[...] = mid + small("pb")
        forward_norm(mid, rs, ("g2", "s2"), c_all, xh2_all, rs2_all)
        ready("f")
        ready("p")

        for i in range(4):
            v = dot(c_all[rs, :], wide(4 + i), NN) + sm_ref[:, fc_cols(i)]
            v2 = v * v
            t = jnp.tanh(v * (GELU_A + (GELU_A * GELU_B) * v2))
            half = 0.5 + 0.5 * t
            ga_all[i, rs, :] = (v * half).astype(BF16)
            slope_all[i, rs, :] = half * (1.0 + v * (1.0 - t) * (GELU_A + (3.0 * GELU_A * GELU_B) * v2))
            acc[...] += dot(ga_all[i, rs, :], proj(i), NN)

    def backward(b):
        base = b * rows
        rs = slice(base, base + rows)
        add_small("pb", colsum(gd_all[rs, :]))
        acc[...] = jnp.zeros_like(acc)
        for i in range(4):
            d = (dot(gd_all[rs, :], proj(i), NT) * slope_all[i, rs, :]).astype(BF16)
            dpre_all[i, rs, :] = d
            sg_ref[:, fc_cols(i)] = sg_ref[:, fc_cols(i)] + colsum(d)
            acc[...] += dot(dpre_all[i, rs, :], wide(4 + i), NT)

        dmid = backward_norm(xh2_all, rs2_all, rs, small("g2"), ("g2", "s2"))
        hid[...] = dmid
        gb_all[rs, :] = dmid.astype(BF16)
        add_small("ob", colsum(gb_all[rs, :]))
        datt[...] = dot(gb_all[rs, :], wide(3), NT).astype(BF16)

        def head_pair(ls, rms, hp):
            outs = [datt[m * n:(m + 1) * n, ls] for m in range(bins)]
            dprobs = [dot(stack(mix_all[2, rm, ls]), outs[m], NT) for m, rm in enumerate(rms)]
            for m, rm in enumerate(rms):
                p = prob_all[(b * bins + m) * (HEADS // 2) + hp]
                dmix_all[2, rm, ls] = unstack(dot(p.reshape(2 * n, n).astype(BF16), outs[m], NN)).astype(BF16)
            dscores = []
            for m in range(bins):
                p = prob_all[(b * bins + m) * (HEADS // 2) + hp]
                dp = dprobs[m].reshape(2, n, n)
                ds = p * (dp - jnp.sum(p * dp, axis=1, keepdims=True))
                dscores.append(ds.reshape(2 * n, n).astype(BF16))
            for m, rm in enumerate(rms):
                ds = dscores[m]
                dmix_all[1, rm, ls] = (unstack(dot(ds, mix_all[0, rm, ls], NN)) * (HD ** -0.5)).astype(BF16)
                dmix_all[0, rm, ls] = (dot(ds, stack(mix_all[1, rm, ls]), TN) * (HD ** -0.5)).astype(BF16)
        pairs(base, head_pair)

        add_small("qb", colsum(dmix_all[0, rs, :]))
        add_small("vb", colsum(dmix_all[2, rs, :]))
        acc[...] = dot(dmix_all[0, rs, :], wide(0), NT)
        acc[...] += dot(dmix_all[1, rs, :], wide(1), NT)
        acc[...] += dot(dmix_all[2, rs, :], wide(2), NT)
        dh = backward_norm(xh1_all, rs1_all, rs, small("g1"), ("g1", "s1"))
        hid[...] = dh
        (gd_all if b == 1 else tg_ref)[0:rows, :] = dh.astype(BF16)

    acc[...] = tok_ref[...].astype(F32)
    forward(0)
    forward(1)
    act_ref[...] = acc[...].astype(BF16)
    hid[...] = cot_ref[...].astype(F32)
    gd_all[rows:2 * rows, :] = cot_ref[...]
    backward(1)
    backward(0)
    emit(a_all, att_all, c_all, ga_all, dmix_all, gb_all, dpre_all, gd_all)


def compute_scratch(rows, width):
    two = 2 * rows
    return [
        pltpu.VMEM((two, width), BF16),
        pltpu.VMEM((two, width), BF16),
        pltpu.VMEM((two, width), BF16),
        pltpu.VMEM((4, two, width), BF16),
        pltpu.VMEM((4, two, width), F32),
        pltpu.VMEM((3, two, width), BF16),
        pltpu.VMEM((two, width), F32),
        pltpu.VMEM((two, width), F32),
        pltpu.VMEM((two, 128), F32),
        pltpu.VMEM((two, 128), F32),
        pltpu.VMEM((2 * HEADS, 2, rows // 2, rows // 2), F32),
        pltpu.VMEM((two, width), BF16),
        pltpu.VMEM((two, width), BF16),
        pltpu.VMEM((4, two, width), BF16),
        pltpu.VMEM((3, two, width), BF16),
        pltpu.VMEM((rows, width), F32),
        pltpu.VMEM((rows, width), F32),
        pltpu.VMEM((rows, width), BF16),
    ]


N_SCR = 18
LIMIT = 64 * 1024 * 1024


def kernel(fast, n_in, n_out, *refs):
    tab, len_ref, tok_ref, cot_ref, sm_in = refs[:5]
    w_in = refs[5:n_in]
    act_ref, tg_ref, sg_ref = refs[n_in:n_in + 3]
    d_out = refs[n_in + 3:n_in + n_out]
    scr = refs[n_in + n_out:n_in + n_out + N_SCR]
    wqo, wf, wp, sm_ref, load_sem, store_sem = refs[n_in + n_out + N_SCR:]
    width = tok_ref.shape[1]
    high = wp.shape[1]
    per = width // high
    core = tab[0, 64]

    def chip_of(kind, who, slot, flip):
        return tab[0, ((kind * 2 + who) * 8 + slot) * 2 + flip]

    whole = {"qo": (wqo, 0), "f": (wf, 1), "p": (wp, 2)}

    def pull(src, dst, part):
        pltpu.make_async_copy(src, dst, load_sem.at[whole[part][1]]).start()

    def pieces():
        for who in range(2):
            c = core if who == 0 else 1 - core
            for flip in range(2):
                for i, offs in enumerate(BATCHES):
                    src = w_in[(who * 2 + flip) * len(BATCHES) + i]
                    for j, off in enumerate(offs):
                        yield c, chip_of(0, who, OFFSETS.index(off), flip), src, PIECE * j

    def pull_first():
        if fast:
            for c, chip, src, k in pieces():
                pull(src.at[k:k + 7], wqo.at[c, chip], "qo")
            return
        sm_ref[...] = sm_in[...]
        for c in range(2):
            for h in range(2):
                src = w_in[0].at[2 * c + h].reshape(16, 3, high, width)
                pull(src, wqo.at[c, :, 1 + 3 * h:4 + 3 * h], "qo")

    def pull_rest():
        if fast:
            for c, chip, src, k in pieces():
                pull(src.at[k + 7:k + 13], wf.at[c, chip], "f")
            for c, chip, src, k in pieces():
                pull(src.at[k + 13:k + 19], wp.at[pl.ds(12 * chip + 6 * c, 6)], "p")
            return
        for c in range(2):
            for h in range(2):
                src = w_in[0].at[4 + 2 * c + h].reshape(16, 3, high, width)
                pull(src, wf.at[c, :, 3 * h:3 * h + 3], "f")
        pull(w_in[1], wp, "p")

    pull_first()
    arrived = set()

    def ready(part):
        if part not in arrived:
            arrived.add(part)
            ref, s = whole[part]
            if part == "qo" and not fast:
                for c in range(2):
                    pltpu.make_async_copy(wqo.at[c, :, 1:7], wqo.at[c, :, 1:7], load_sem.at[s]).wait()
            else:
                pltpu.make_async_copy(ref, ref, load_sem.at[s]).wait()
            if part == "qo":
                pull_rest()
                if fast:
                    unpack_small()

    def one_hot(v, size):
        return (lax.broadcasted_iota(jnp.int32, (size, width), 0) == sm_in[v:v + 1, :]).astype(BF16)

    def owned(v):
        return lax.broadcasted_iota(jnp.int32, (32, width), 0) == sm_in[12 + v:13 + v, :]

    def first_rows():
        line = lax.broadcasted_iota(jnp.int32, (32, 32 * high), 0)
        return (lax.broadcasted_iota(jnp.int32, (32, 32 * high), 1) == high * line).astype(BF16)

    lanes = 384

    def small_parts():
        base, v = 0, 0
        for rows in SMALL_ROWS:
            for _ in range(rows):
                yield v, base, rows * PART
                v += 1
            base += rows * PART

    def unpack_small():
        tiles = wqo[:, :, 0].reshape(32 * high, width)
        packed = dot(first_rows(), tiles[:, :lanes], NN).astype(BF16)
        for v, base, size in small_parts():
            full = jnp.where(owned(v), dot(packed[:, base:base + size], one_hot(v, size), NN), 0.0)
            sm_ref[:, v * width:(v + 1) * width] = jnp.sum(full, axis=0, keepdims=True)

    def pack_small():
        packed = jnp.zeros((32, lanes), F32)
        for v, base, size in small_parts():
            mine = jnp.where(owned(v), sg_ref[:, v * width:(v + 1) * width], 0.0).astype(BF16)
            part = dot(mine, one_hot(v, size), NT).astype(BF16)
            shift = lax.broadcasted_iota(jnp.int32, (size, lanes), 1) - lax.broadcasted_iota(jnp.int32, (size, lanes), 0)
            packed += dot(part, (shift == base).astype(BF16), NN)
        tiles = dot(first_rows(), packed.astype(BF16), TN).astype(BF16)
        wqo[:, :, 0, :, :lanes] = tiles.reshape(2, 16, high, lanes)

    def view(k):
        c, h = k % 4 // 2, k % 2
        return wqo.at[c, :, 1 + 3 * h:4 + 3 * h] if k < 4 else wf.at[c, :, 3 * h:3 * h + 3]

    def load_qf(k):
        return view(k)[...].reshape(width, width)

    def load_p(i):
        return wp[pl.ds(i * per, per)].reshape(width, width)

    def drain(ref, s):
        pltpu.make_async_copy(ref, ref, store_sem.at[s]).wait()

    def push(src, dst, s):
        pltpu.make_async_copy(src, dst, store_sem.at[s]).start()

    def product(left, right, out):
        half = width // 2
        for r in range(2):
            value = dot(left[:, r * half:(r + 1) * half], right[...], TN).astype(BF16)
            tiles = out.shape[0] // 2
            out[r * tiles:(r + 1) * tiles] = value.reshape((tiles,) + out.shape[1:])

    def keep_refs(slot, flip):
        for i, offs in enumerate(BATCHES):
            if OFFSETS[slot] in offs:
                at = offs.index(OFFSETS[slot])
                return d_out[3 * i + flip].at[at], d_out[3 * i + 2].at[flip, at]

    def half_stored(c, who, slot, flip, dst):
        @pl.when(core == (c if who == 0 else 1 - c))
        def _():
            push(wqo.at[c, chip_of(1, who, slot, flip)], dst.at[0:7], 2)

    def targets():
        for slot in range(8):
            for flip in range(2):
                for who, dst in enumerate(keep_refs(slot, flip)):
                    yield core if who == 0 else 1 - core, chip_of(1, who, slot, flip), dst

    def emit(a_all, att_all, c_all, ga_all, dmix_all, gb_all, dpre_all, gd_all):
        for i in range(4):
            product(ga_all.at[i], gd_all, wp.at[i * per:(i + 1) * per])
        if fast:
            for c, chip, dst in targets():
                push(wp.at[pl.ds(12 * chip + 6 * c, 6)], dst.at[13:19], 0)
        else:
            push(wp, d_out[1], 0)
        for i in range(4):
            product(c_all, dpre_all.at[i], view(4 + i))
        if fast:
            for c, chip, dst in targets():
                push(wf.at[c, chip], dst.at[7:13], 1)
            pack_small()
        product(att_all, gb_all, view(3))
        for i in (2, 0, 1):
            product(a_all, dmix_all.at[i], view(i))
            if fast and i != 0:
                for slot in range(8):
                    for flip in range(2):
                        for who, dst in enumerate(keep_refs(slot, flip)):
                            half_stored(1 if i == 2 else 0, who, slot, flip, dst)
        if fast:
            drain(wqo, 2)
        else:
            for k in range(8):
                push(view(k), d_out[0].at[k].reshape(16, 3, high, width), 1 if k >= 4 else 2)
            for c in range(2):
                drain(wqo.at[c, :, 1:7], 2)
        drain(wf, 1)
        drain(wp, 0)

    compute(len_ref, tok_ref, cot_ref, sm_ref, act_ref, tg_ref, sg_ref, scr, (load_qf, load_p), ready, emit)


def run_kernel(fast, table, lengths, tokens, cotangent, smalls, w_in, d_shapes):
    rows, width = tokens.shape
    high = 16
    per = width // high
    n_in = 5 + len(w_in)
    smem = pl.BlockSpec(memory_space=pltpu.SMEM)
    vmem = pl.BlockSpec(memory_space=pltpu.VMEM)
    hbm = pl.BlockSpec(memory_space=pl.ANY)
    out_shape = [
        jax.ShapeDtypeStruct((rows, width), BF16),
        jax.ShapeDtypeStruct((rows, width), BF16),
        jax.ShapeDtypeStruct((1, 12 * width), F32),
    ] + [jax.ShapeDtypeStruct(s, BF16) for s in d_shapes]
    return pl.pallas_call(
        functools.partial(kernel, fast, n_in, len(out_shape)),
        out_shape=out_shape,
        in_specs=[smem, smem, vmem, vmem, vmem] + [hbm] * len(w_in),
        out_specs=[vmem, vmem, vmem] + [hbm] * len(d_shapes),
        scratch_shapes=compute_scratch(rows, width) + [
            pltpu.VMEM((2, 16, 7, high, width), BF16),
            pltpu.VMEM((2, 16, 6, high, width), BF16),
            pltpu.VMEM((4 * per, high, width), BF16),
            pltpu.VMEM((1, 12 * width), F32),
            pltpu.SemaphoreType.DMA((3,)),
            pltpu.SemaphoreType.DMA((3,)),
        ],
        compiler_params=pltpu.CompilerParams(vmem_limit_bytes=LIMIT),
        cost_estimate=pl.CostEstimate(flops=22_000_000_000, bytes_accessed=32_000_000, transcendentals=4_000_000),
        name="blocks",
    )(table, lengths, tokens, cotangent, smalls, *w_in)


VECTORS = ("g1", "s1", "qv", "ob", "g2", "s2", "fb", "pb")


def spread(vectors, count, me):
    parts = []
    for v in vectors:
        mine = v.astype(BF16).astype(F32)
        owner = lax.broadcasted_iota(jnp.int32, (count, v.shape[0]), 0)
        parts.append(jnp.where(owner == me, mine[None, :], 0.0).reshape(-1))
    return jnp.concatenate(parts)


def own_parts(packed, sizes, count, me):
    parts, base = [], 0
    for size in sizes:
        parts.append(lax.dynamic_slice(packed, (base + me * size,), (size,)))
        base += size * count
    return parts


def total_small(packed, steps):
    for step in steps:
        packed = add_swapped(packed, step)
    return packed


def add_swapped(packed, step):
    return packed + lax.ppermute(packed, *step)


def swap_steps(sizes):
    steps = []
    for axis, size in sizes:
        bit = 1
        while bit < size:
            steps.append((axis, [(i, i ^ bit) for i in range(size)]))
            bit *= 2
    return steps


def both_ways():
    cw, ccw, swap, pair = ring_pairs(1), ring_pairs(-1), swap_pairs(), core_pairs()
    return tuple(functools.partial(lax.ppermute, axis_name=AXES, perm=p) for p in (cw, ccw, swap, pair))


PLAN = (
    ("s0", 0, 0),
    ("s1", 1, 2),
    ("s2", 2, 3),
    ("s3", 3, 4),
    ("s4", 4, 4),
    ("c0", 0, 0),
    ("c1", 2, 2),
    ("c2", 4, 4),
    ("c3", 4, 4),
    ("c4", 4, 5),
    ("cs0", 1, 2),
    ("cs1", 3, 3),
    ("cs2", 3, 4),
    ("cs3", 4, 5),
    ("cs4", 5, 5),
)


def gather_pieces(piece, table):
    cw, ccw, swap, pair = both_ways()
    half = piece.shape[0] // 2
    have = {"p0": piece}
    right = left = piece
    for stage in range(6):
        arrivals = {}
        if stage < 4:
            if stage == 3:
                right, left = right[:half], left[half:]
            arrivals = {"right": cw(right), "left": ccw(left)}
        for what, first, _ in PLAN:
            if first == stage:
                have[what] = swap(have["p" + what[1:]]) if what[0] == "s" else pair(have[what[1:] if what[1] == "s" else "p" + what[1:]])
        if stage == 5:
            break
        arrivals |= {what: have[what] for what, _, last in PLAN if last == stage}
        if stage == 4:
            arrivals["table"] = table
        have |= dict(zip(arrivals, lax.optimization_barrier(tuple(arrivals.values()))))
        if stage < 4:
            right, left = have["right"], have["left"]
            have[f"p{stage + 1}"] = jnp.concatenate([right, left])
    return [have[f"{kind}{k}"] for kind in ("p", "s", "c", "cs") for k in (4, 3, 2, 1, 0)], have["table"]


def scatter_sums(outs):
    cw, ccw, swap, pair = both_ways()
    stage = lax.optimization_barrier

    def add(a, b):
        return (a.astype(F32) + b.astype(F32)).astype(BF16)

    kept, flipped, sent = outs[0::3], outs[1::3], list(outs[2::3])
    got = [pair(sent[0]), pair(sent[1]), pair(sent[2]), None, None]
    moved = [None] * 5

    def total(i):
        return kept[i].astype(F32) + got[i][0].astype(F32) + moved[i].astype(F32)

    moved[0] = swap(add(flipped[0], got[0][1]))
    sent[3], got[0] = stage((sent[3], got[0]))
    got[3] = pair(sent[3])
    moved[1] = swap(add(flipped[1], got[1][1]))
    sent[4], got[2] = stage((sent[4], got[2]))
    got[4] = pair(sent[4])
    moved[0], got[2], got[3] = stage((moved[0], got[2], got[3]))
    first = total(0)[0].astype(BF16)
    half = first.shape[0] // 2
    right, left = cw(first[:half]), ccw(first[half:])
    moved[2] = swap(add(flipped[2], got[2][1]))
    moved[1], right, left = stage((moved[1], right, left))
    second = total(1)
    right, left = jnp.concatenate([right, jnp.zeros_like(left)]), jnp.concatenate([jnp.zeros_like(right), left])
    right = cw((second[0] + right.astype(F32)).astype(BF16))
    left = ccw((second[1] + left.astype(F32)).astype(BF16))
    moved[3] = swap(add(flipped[3], got[3][1]))
    moved[2], right, left = stage((moved[2], right, left))
    third = total(2)
    right = cw((third[0] + right.astype(F32)).astype(BF16))
    left = ccw((third[1] + left.astype(F32)).astype(BF16))
    moved[4] = swap(add(flipped[4], got[4][1]))
    moved[3], right, left = stage((moved[3], right, left))
    fourth = total(3)
    right = cw((fourth[0] + right.astype(F32)).astype(BF16))
    left = ccw((fourth[1] + left.astype(F32)).astype(BF16))
    return total(4)[0] + right.astype(F32) + left.astype(F32)


def body(sizes, tokens, lengths, ln1_gain, ln1_shift, w_qkv, qv_bias, w_out, out_bias, ln2_gain, ln2_shift,
         w_fc, fc_bias, w_proj, proj_bias, cotangent):
    dp, fsdp = sizes
    count = dp * fsdp
    me = lax.axis_index("dp") * fsdp + lax.axis_index("fsdp")
    bins, n, width = tokens.shape
    fast = (dp, fsdp) == (4, 8)
    vectors = (ln1_gain, ln1_shift, qv_bias, out_bias, ln2_gain, ln2_shift, fc_bias, proj_bias)
    steps = swap_steps((("fsdp", fsdp), ("dp", dp)))
    part = w_qkv.shape[0]
    wide = jnp.stack([
        w_qkv[:, :width], w_qkv[:, width:2 * width], w_qkv[:, 2 * width:], w_out,
        w_fc[:, :width], w_fc[:, width:2 * width], w_fc[:, 2 * width:3 * width], w_fc[:, 3 * width:],
    ]).astype(BF16)
    proj = w_proj.astype(BF16)
    flat = (lengths.reshape(bins, -1), tokens.reshape(-1, width), cotangent.reshape(-1, width))
    if fast:
        core = me % 2
        chips = jnp.array(TABLE, jnp.int32)
        table = lax.dynamic_slice(chips, (me, 0), (1, chips.shape[1]))
        halves = wide.reshape(2, 2, 2, part, width)
        mine = jnp.where(core == 0, halves[:, 0], halves[:, 1])
        theirs = jnp.where(core == 0, halves[:, 1], halves[:, 0])
        other = lax.ppermute(theirs, AXES, core_pairs())
        both = jnp.where(core == 0, jnp.concatenate([mine, other], 2), jnp.concatenate([other, mine], 2))
        row = jnp.concatenate(vectors).astype(BF16)
        row = jnp.pad(row[None, None, :], ((0, 0), (0, 15), (0, width - row.shape[0])))
        piece = jnp.concatenate([row, both.reshape(12, 16, width), proj.reshape(6, 16, width)])
        pieces, table = gather_pieces(piece, table)
        shape = piece.shape
        d_shapes = []
        for offs in BATCHES:
            k = len(offs)
            d_shapes += [(k,) + shape, (k,) + shape, (2, k) + shape]
        act, tgrad, _, *outs = run_kernel(True, table, *flat, small_spots(), pieces, d_shapes)
        total = scatter_sums(outs)
        square = total[1:13].reshape(4, 2 * part, width)
        high = square[:, :part], square[:, part:]
        own = jnp.where(core == 0, high[0], high[1])
        got = lax.ppermute(jnp.where(core == 0, high[1], high[0]), AXES, core_pairs())
        own, got = own.reshape(2, 2, part, width), got.reshape(2, 2, part, width)
        blocks = jnp.where(core == 0, jnp.concatenate([own, got], 1), jnp.concatenate([got, own], 1))
        blocks = blocks.reshape(8, part, width)
        d_proj = total[13:].reshape(w_proj.shape)
        small, base = [], 0
        for v in vectors:
            small.append(total[0, 0, base:base + v.shape[0]])
            base += v.shape[0]
    else:
        table = jnp.zeros((1, 65), jnp.int32)
        w_all = lax.all_gather(wide, AXES, axis=1, tiled=True)
        p_all = lax.all_gather(proj, AXES, axis=0, tiled=True).reshape(-1, 16, width)
        packed = spread(vectors, count, me)
        blocks_all = w_all.reshape((8, -1) + p_all.shape[1:])
        act, tgrad, small_sums, d_wide, d_p = run_kernel(
            False, table, *flat, total_small(packed, steps).reshape(1, -1), [blocks_all, p_all],
            [blocks_all.shape, p_all.shape])
        blocks = lax.psum_scatter(d_wide.reshape(w_all.shape), AXES, scatter_dimension=1, tiled=True).astype(F32)
        d_proj = lax.psum_scatter(d_p.reshape(-1, width), AXES, scatter_dimension=0, tiled=True).astype(F32)
        small = own_parts(total_small(small_sums.reshape(-1), steps), [v.shape[0] for v in vectors], count, me)
    g1, s1, qv, ob, g2, s2, fb, pb = small
    d_qkv = jnp.concatenate([blocks[0], blocks[1], blocks[2]], axis=1)
    d_fc = jnp.concatenate([blocks[4], blocks[5], blocks[6], blocks[7]], axis=1)
    return (act.reshape(tokens.shape), tgrad.reshape(tokens.shape), g1, s1, d_qkv, qv, blocks[3], ob, g2, s2,
            d_fc, fb, d_proj, pb)


def make_table():
    gather, scatter = relative_chips(-1), relative_chips(1)
    rows = []
    for chip in range(16):
        for core in range(2):
            row = []
            for table in (gather, scatter):
                for who in range(2):
                    for slot in range(8):
                        row += table[chip][core ^ who][slot]
            rows.append(row + [core])
    return rows


TABLE = make_table()


def small_spots():
    spots, owners = [], []
    for rows in SMALL_ROWS:
        size = rows * PART
        for r in range(rows):
            spots.append([(r * 768 + col) % size for col in range(768)])
            owners.append([(r * 768 + col) // size % 2 * 16 + (r * 768 + col) // size // 2 for col in range(768)])
    return jnp.array(spots + owners, jnp.int32)


def solution(mesh):
    both = P(AXES)
    rows = P(None, AXES, None)
    matrix = P(AXES, None)
    weights = (both, both, matrix, both, matrix, both, both, both, matrix, both, matrix, both)
    return jax.shard_map(
        functools.partial(body, (mesh.shape["dp"], mesh.shape["fsdp"])),
        mesh=mesh,
        in_specs=(rows, rows) + weights + (rows,),
        out_specs=(rows, rows) + weights,
        check_vma=False,
    )
```
